32 devices in a mesh: section: 4 (over x, core), fsdp: 2 (over y), tensor: 4 (over z).
Axes of the slice: x: 2, y: 2, z: 4, core: 2. Of those that a mesh axis runs over, the one named last changes fastest.
Arguments:
- entering: bfloat16 [4, 1024, 2048], P('section', 'fsdp', 'tensor'), may hold values from -8 to 8
- w_query: bfloat16 [4, 2048, 4096], P('section', 'fsdp', 'tensor'), may hold values from -0.125 to 0.125
- w_keyval: bfloat16 [4, 2048, 4, 256], P('section', 'fsdp', 'tensor'), may hold values from -0.125 to 0.125
- w_out: bfloat16 [4, 4096, 2048], P('section', 'tensor', 'fsdp'), may hold values from -0.09375 to 0.09375
Outputs:
- leaving: bfloat16 [4, 1024, 2048], P('section', 'fsdp', 'tensor')
The draws below stay inside these ranges and needn't reach their ends.
All inputs are finite; a program needn't handle non-finite values.
Results may differ from the reference program's by a relative error of at most 0.0055.
Values may be sent and summed in bfloat16 or wider, within the bound.
No kernel may reach another device: no remote copies, remote signals or barrier semaphores. Data moves between devices by JAX's collectives and lax.ppermute only.
A program may use at most 128 MiB of HBM per device.

```python
import math
import jax
import jax.numpy as jnp
from jax import lax

D = 2048
HEADS = 32
KV_HEADS = 4
HEAD_DIM = 128
SEQ = 512
SECTIONS = 4
TOKENS = 1024
N_FSDP = 2
N_TENSOR = 4


def draw_entering(key, part):
    first_key = jax.random.fold_in(key, 0)
    values = jax.random.normal(first_key, (SECTIONS, TOKENS, D), jnp.float32)
    return jnp.clip(values, -8.0, 8.0).astype(jnp.bfloat16)


def block_scale(key, shape, shards, low, high):
    factor_of = 1.0
    for position, blocks in shards:
        draws = jax.random.uniform(jax.random.fold_in(jax.random.fold_in(key, 6), position), (blocks,), jnp.float32, low / len(shards), high / len(shards))
        factor_of = factor_of * jnp.repeat(jnp.exp(draws), shape[position] // blocks).reshape((-1,) + (1,) * (len(shape) - 1 - position))
    return factor_of


def gaussian(key, extent, spread, reach, pieces=(), kind=jnp.bfloat16):
    array = jax.random.normal(key, extent, jnp.float32) * spread
    if len(pieces) > 0:
        array = block_scale(key, extent, pieces, -0.22, 0.18) * array
    return jnp.clip(array, min=-reach, max=reach).astype(kind)


def setup_inputs(seed: int = 0) -> dict:
    seeds = jax.random.split(jax.random.key(seed), 5)
    entering = draw_entering(jax.random.fold_in(seeds[4], 71), 0)
    w_query = gaussian(seeds[1], (SECTIONS, D, HEADS * HEAD_DIM), D ** -0.5, 0.125, ((0, 4), (1, 2), (2, 4)))
    w_keyval = gaussian(seeds[2], (SECTIONS, D, KV_HEADS, 2 * HEAD_DIM), D ** -0.5, 0.125, ((0, 4), (1, 2), (2, 4)))
    w_out = gaussian(seeds[3], (SECTIONS, HEADS * HEAD_DIM, D), (HEADS * HEAD_DIM) ** -0.5, 0.09375, ((0, 4), (1, 4), (2, 2)))
    return {"entering": entering, "w_query": w_query, "w_keyval": w_keyval, "w_out": w_out}


EPSILON = 1e-06
ROPE_BASE = 1000000.0
BEFORE_SHARE = 0.6
AFTER_SHARE = 0.4

def rope_tables(length, width):
    half_width = width // 2
    exponent = jnp.arange(half_width, dtype=jnp.float32) * (2.0 / width)
    inverse = jnp.exp(-exponent * math.log(ROPE_BASE))
    angles = jnp.arange(length, dtype=jnp.float32)[:, None] * inverse[None, :]
    return (jnp.cos(angles)[:, None, :], jnp.sin(angles)[:, None, :])

def head_norm_rope(vectors, cosine, sine):
    meansq = lax.optimization_barrier(jnp.mean(vectors * vectors, axis=-1, keepdims=True))
    normed = vectors * lax.rsqrt(meansq + EPSILON)
    half_width = vectors.shape[-1] // 2
    first_half = normed[..., :half_width]
    second_half = normed[..., half_width:]
    return jnp.concatenate([first_half * cosine - second_half * sine, second_half * cosine + first_half * sine], axis=-1)

def attend(packed):
    queries, keys, values = packed
    length = queries.shape[0]
    scale = 1.0 / math.sqrt(HEAD_DIM)
    scores = jnp.einsum('qkgd,pkd->kgqp', queries.astype(jnp.float32), keys.astype(jnp.float32)) * scale
    positions = jnp.arange(length)
    causal = positions[:, None] >= positions[None, :]
    expo = jnp.where(causal[None, None], jnp.exp(scores - math.sqrt(HEAD_DIM)), 0.0)
    weights = (expo / lax.optimization_barrier(jnp.sum(expo, axis=-1, keepdims=True))).astype(jnp.bfloat16)
    mixed = jnp.einsum('kgqp,pkd->qkgd', weights.astype(jnp.float32), values.astype(jnp.float32))
    return mixed.astype(jnp.bfloat16).reshape(length, -1)

def sublayer(rows, query_weight, keyval_weight, out_weight):
    rows_float = rows.astype(jnp.float32)
    meansq = lax.optimization_barrier(jnp.mean(rows_float * rows_float, axis=-1, keepdims=True))
    normed = (rows_float * lax.rsqrt(meansq + EPSILON)).astype(jnp.bfloat16)
    group_size = HEADS // KV_HEADS
    query_raw = jnp.dot(normed, query_weight, preferred_element_type=jnp.float32)
    query_raw = query_raw.reshape(N_FSDP, SEQ, KV_HEADS, group_size, HEAD_DIM)
    keyval_raw = jnp.dot(normed, keyval_weight.reshape(D, -1), preferred_element_type=jnp.float32)
    keyval_raw = keyval_raw.reshape(N_FSDP, SEQ, KV_HEADS, 2 * HEAD_DIM)
    cosine, sine = rope_tables(SEQ, HEAD_DIM)
    queries = head_norm_rope(query_raw, cosine[:, :, None, :], sine[:, :, None, :]).astype(jnp.bfloat16)
    keys = head_norm_rope(keyval_raw[..., :HEAD_DIM], cosine, sine).astype(jnp.bfloat16)
    values = keyval_raw[..., HEAD_DIM:].astype(jnp.bfloat16)
    mixed = lax.map(attend, (queries, keys, values))
    mixed = mixed.reshape(TOKENS, HEADS * HEAD_DIM)
    shard_width = HEADS * HEAD_DIM // N_TENSOR
    total = jnp.zeros((TOKENS, D), jnp.float32)
    for shard in range(N_TENSOR):
        partial_term = jnp.dot(mixed[:, shard * shard_width:(shard + 1) * shard_width], out_weight[shard * shard_width:(shard + 1) * shard_width], preferred_element_type=jnp.float32).astype(jnp.bfloat16)
        partial_term = lax.optimization_barrier(partial_term)
        total = total + partial_term.astype(jnp.float32)
    return (rows_float + total).astype(jnp.bfloat16)

def rebuild(weights, section):
    lower_part = weights[(section - 1) % SECTIONS].astype(jnp.float32)
    upper_part = weights[(section + 1) % SECTIONS].astype(jnp.float32)
    return (BEFORE_SHARE * lower_part + AFTER_SHARE * upper_part).astype(jnp.bfloat16)

def reference(entering, w_query, w_keyval, w_out):
    results = []
    for section in range(SECTIONS):
        query_weight = rebuild(w_query, section)
        keyval_weight = rebuild(w_keyval, section)
        out_weight = rebuild(w_out, section)
        results.append(sublayer(entering[section], query_weight, keyval_weight, out_weight))
    return jnp.stack(results)
```

```python
import functools
import math

import jax
import jax.numpy as jnp
from jax import lax
from jax.experimental import pallas as pl
from jax.experimental.pallas import tpu as pltpu
from jax.sharding import PartitionSpec as P

HEAD_DIM = 128
EPSILON = 1e-06
ROPE_BASE = 1000000.0
BEFORE_SHARE = 0.6
AFTER_SHARE = 0.4
LANES = 128
VMEM_BYTES = 48 * 1024 * 1024
QUERY_CHUNKS = 4
OUT_CHUNKS = 4

SMEM = pl.BlockSpec(memory_space=pltpu.SMEM)
VMEM = pl.BlockSpec(memory_space=pltpu.VMEM)


def params():
    return pltpu.CompilerParams(vmem_limit_bytes=VMEM_BYTES)


def rope_tables(length, width):
    half_width = width // 2
    exponent = jnp.arange(half_width, dtype=jnp.float32) * (2.0 / width)
    inverse = jnp.exp(-exponent * math.log(ROPE_BASE))
    angles = jnp.arange(length, dtype=jnp.float32)[:, None] * inverse[None, :]
    cosine, sine = jnp.cos(angles), jnp.sin(angles)
    return jnp.concatenate([cosine, cosine], axis=1), jnp.concatenate([-sine, sine], axis=1)


def combine_kernel(shares, near, far, out):
    mixed = shares[0] * near[...].astype(jnp.float32) + shares[1] * far[...].astype(jnp.float32)
    out[...] = mixed.astype(out.dtype)


def combine(shares, near, far, near_block, width):
    rows, columns = far.shape
    pieces = columns // width
    step = min(rows, 512)
    return pl.pallas_call(
        combine_kernel,
        out_shape=jax.ShapeDtypeStruct(far.shape, far.dtype),
        grid=(rows // step, pieces),
        in_specs=[
            SMEM,
            pl.BlockSpec((step, width), lambda i, j: (i, near_block(j))),
            pl.BlockSpec((step, width), lambda i, j: (i, j)),
        ],
        out_specs=pl.BlockSpec((step, width), lambda i, j: (i, j)),
        compiler_params=params(),
        cost_estimate=pl.CostEstimate(
            flops=3 * far.size, bytes_accessed=6 * far.size, transcendentals=0
        ),
    )(shares, near, far)


def project(ids, blocks, own, other, whole):
    half = own.shape[0]
    mine, place, count = ids[0], ids[1], len(blocks)
    whole[pl.ds(pl.multiple_of(mine * half, half), half), :] = own[...]
    whole[pl.ds(pl.multiple_of((1 - mine) * half, half), half), :] = other[...]
    total = None
    for k, block in enumerate(blocks):
        width = block.shape[1]
        owner = lax.rem(place - k + count, count)
        rows = pl.ds(pl.multiple_of(owner * width, width), width)
        term = jnp.dot(block[...], whole[rows, :], preferred_element_type=jnp.float32)
        total = term if total is None else total + term
    return total


def norm_rope(vectors, cosine, signed_sine):
    meansq = jnp.mean(vectors * vectors, axis=-1, keepdims=True)
    normed = vectors * lax.rsqrt(meansq + EPSILON)
    return normed * cosine + pltpu.roll(normed, HEAD_DIM // 2, 1) * signed_sine


def keyval_kernel(count, ids, *refs):
    blocks = refs[:count]
    own, other, cosine, sine, keys, values, scales, whole = refs[count:]
    total = 0.0
    features = 0
    for block in blocks:
        rows = block[...].astype(jnp.float32)
        total = total + jnp.sum(rows * rows, axis=-1, keepdims=True)
        features += block.shape[1]
    scale = lax.rsqrt(total / features + EPSILON)
    raw = project(ids, blocks, own, other, whole) * scale
    keys[...] = norm_rope(raw[:, :HEAD_DIM], cosine[...], sine[...]).astype(keys.dtype)
    values[...] = raw[:, HEAD_DIM:].astype(values.dtype)
    scales[...] = jnp.broadcast_to(scale, scales.shape)


def keyval(ids, blocks, own, other, cosine, sine):
    length = blocks[0].shape[0]
    features = sum(b.shape[1] for b in blocks)
    head = jax.ShapeDtypeStruct((length, HEAD_DIM), jnp.bfloat16)
    return pl.pallas_call(
        functools.partial(keyval_kernel, len(blocks)),
        out_shape=(head, head, jax.ShapeDtypeStruct((length, LANES), jnp.float32)),
        in_specs=[SMEM] + [VMEM] * (len(blocks) + 4),
        out_specs=(VMEM,) * 3,
        scratch_shapes=[pltpu.VMEM((features, own.shape[1]), own.dtype)],
        compiler_params=params(),
        cost_estimate=pl.CostEstimate(
            flops=2 * length * features * own.shape[1],
            bytes_accessed=2 * features * (length + own.shape[1]),
            transcendentals=0,
        ),
    )(ids, *blocks, own, other, cosine, sine)


def attend_kernel(count, ids, *refs):
    blocks = refs[:count]
    own, other, keys, values, scales, cosine, sine, mixed, whole = refs[count:]
    raw = project(ids, blocks, own, other, whole)
    length = raw.shape[0]
    rows = length // 2 if length % 16 == 0 else length
    scale = scales[:, :1]
    for head in range(raw.shape[1] // HEAD_DIM):
        columns = slice(head * HEAD_DIM, (head + 1) * HEAD_DIM)
        query = norm_rope(raw[:, columns] * scale, cosine[...], sine[...]).astype(jnp.bfloat16)
        for first in range(0, length, rows):
            last = first + rows
            scores = lax.dot_general(
                query[first:last],
                keys[:last, :],
                (((1,), (1,)), ((), ())),
                preferred_element_type=jnp.float32,
            )
            expo = jnp.exp(scores * (1.0 / math.sqrt(HEAD_DIM)) - math.sqrt(HEAD_DIM))
            at = first + lax.broadcasted_iota(jnp.int32, expo.shape, 0)
            expo = jnp.where(lax.broadcasted_iota(jnp.int32, expo.shape, 1) <= at, expo, 0.0)
            total = jnp.sum(expo, axis=-1, keepdims=True)
            product = jnp.dot(
                expo.astype(jnp.bfloat16), values[:last, :], preferred_element_type=jnp.float32
            )
            mixed[first:last, columns] = (product / total).astype(mixed.dtype)


def attend(ids, blocks, own, other, keys, values, scales, cosine, sine):
    length = blocks[0].shape[0]
    features = sum(b.shape[1] for b in blocks)
    width = own.shape[1]
    return pl.pallas_call(
        functools.partial(attend_kernel, len(blocks)),
        out_shape=jax.ShapeDtypeStruct((length, width), jnp.bfloat16),
        in_specs=[SMEM] + [VMEM] * (len(blocks) + 7),
        out_specs=VMEM,
        scratch_shapes=[pltpu.VMEM((features, width), own.dtype)],
        compiler_params=params(),
        cost_estimate=pl.CostEstimate(
            flops=2 * length * features * width + 3 * length * length * width,
            bytes_accessed=2 * features * (length + width),
            transcendentals=length * length * width // HEAD_DIM,
        ),
    )(ids, *blocks, own, other, keys, values, scales, cosine, sine)


def partial_kernel(count, parts, ids, *refs):
    mixed = refs[:parts]
    own, other = refs[parts : parts + 2]
    outs = refs[parts + 2 : parts + 2 + count]
    by_owner = refs[-1]
    mine, place = ids[0], ids[1]
    width = by_owner.shape[2]
    per_half = count // 2
    for half, weights in ((mine, own), (1 - mine, other)):
        total = None
        depth = 0
        for part in mixed:
            rows = slice(depth, depth + part.shape[1])
            depth += part.shape[1]
            term = jnp.dot(part[...], weights[rows, :], preferred_element_type=jnp.float32)
            total = term if total is None else total + term
        for piece in range(per_half):
            by_owner[half * per_half + piece] = total[
                :, piece * width : (piece + 1) * width
            ].astype(by_owner.dtype)
    for k in range(count):
        outs[k][...] = by_owner[lax.rem(place + k, count)]


def partials(ids, mixed, own, other, count):
    length = mixed[0].shape[0]
    width = 2 * own.shape[1] // count
    piece = jax.ShapeDtypeStruct((length, width), jnp.bfloat16)
    return pl.pallas_call(
        functools.partial(partial_kernel, count, len(mixed)),
        out_shape=(piece,) * count,
        in_specs=[SMEM] + [VMEM] * (len(mixed) + 2),
        out_specs=(VMEM,) * count,
        scratch_shapes=[pltpu.VMEM((count, length, width), jnp.bfloat16)],
        compiler_params=params(),
        cost_estimate=pl.CostEstimate(
            flops=4 * length * own.size,
            bytes_accessed=4 * own.size + 2 * length * (own.shape[0] + 2 * own.shape[1]),
            transcendentals=0,
        ),
    )(ids, *mixed, own, other)


def leave_kernel(count, chunks, rows, *refs):
    out = refs[-1]
    width = refs[0].shape[1]
    for chunk in range(chunks):
        columns = slice(chunk * width, (chunk + 1) * width)
        pieces = refs[chunk * count : (chunk + 1) * count]
        total = pieces[0][...].astype(jnp.float32)
        for piece in pieces[1:]:
            total = total + piece[...].astype(jnp.float32)
        out[:, columns] = (rows[:, columns].astype(jnp.float32) + total).astype(out.dtype)


def leave(rows, pieces):
    flat = [piece for chunk in pieces for piece in chunk]
    return pl.pallas_call(
        functools.partial(leave_kernel, len(pieces[0]), len(pieces)),
        out_shape=jax.ShapeDtypeStruct(rows.shape, rows.dtype),
        in_specs=[VMEM] * (1 + len(flat)),
        out_specs=VMEM,
        compiler_params=params(),
        cost_estimate=pl.CostEstimate(
            flops=(1 + len(pieces[0])) * rows.size,
            bytes_accessed=2 * rows.size * (2 + len(pieces[0])),
            transcendentals=0,
        ),
    )(rows, *flat)


def permute(array, axis, source):
    count = lax.axis_size(axis)
    return lax.ppermute(array, axis, [(source(i) % count, i) for i in range(count)])


def from_near(array):
    return permute(array, "section", lambda i: i ^ 1)


def from_far(array):
    return permute(array, "section", lambda i: i + 1 if i % 2 else i - 1)


def from_other_half(array):
    return permute(array, "fsdp", lambda i: i ^ 1)


def body(entering, w_query, w_keyval, w_out):
    count = lax.axis_size("tensor")
    section = lax.axis_index("section")
    ids = jnp.stack([lax.axis_index("fsdp"), lax.axis_index("tensor")]).astype(jnp.int32)
    shares = jnp.where(
        section % 2 == 0,
        jnp.array([AFTER_SHARE, BEFORE_SHARE], jnp.float32),
        jnp.array([BEFORE_SHARE, AFTER_SHARE], jnp.float32),
    )
    rows = entering[0]
    length = rows.shape[0]
    own_query = w_query[0]
    own_keyval = w_keyval.reshape(w_keyval.shape[1], -1)
    own_out = w_out[0]
    query_width = own_query.shape[1] // QUERY_CHUNKS
    halves = count // 2
    quarter = own_out.shape[1] // halves
    out_width = quarter // OUT_CHUNKS

    far_keyval = from_far(own_keyval)
    near_keyval = from_near(own_keyval)
    blocks = [rows] + [permute(rows, "tensor", lambda i, k=k: i - k) for k in range(1, count)]
    near_query = from_near(own_query)
    near_out = from_near(own_out)
    far_query = [
        from_far(own_query[:, c * query_width : (c + 1) * query_width])
        for c in range(QUERY_CHUNKS)
    ]
    far_out = [
        from_far(
            jnp.concatenate(
                [
                    own_out[:, h * quarter + c * out_width : h * quarter + (c + 1) * out_width]
                    for h in range(halves)
                ],
                axis=1,
            )
        )
        for c in range(OUT_CHUNKS)
    ]
    cosine, sine = rope_tables(length, HEAD_DIM)

    keyval_own = combine(shares, near_keyval, far_keyval, lambda j: 0, own_keyval.shape[1])
    keyval_other = from_other_half(keyval_own)
    query_own, query_other = [], []
    for c in range(QUERY_CHUNKS):
        query_own.append(
            combine(shares, near_query, far_query[c], lambda j, c=c: c, query_width)
        )
        query_other.append(from_other_half(query_own[c]))
    out_own, out_other = [], []
    for c in range(OUT_CHUNKS):
        out_own.append(
            combine(
                shares, near_out, far_out[c], lambda j, c=c: j * OUT_CHUNKS + c, out_width
            )
        )
        out_other.append(from_other_half(out_own[c]))

    keys, values, scales = keyval(ids, blocks, keyval_own, keyval_other, cosine, sine)
    mixed = [
        attend(
            ids, blocks, query_own[c], query_other[c], keys, values, scales, cosine, sine
        )
        for c in range(QUERY_CHUNKS)
    ]
    pieces = []
    for c in range(OUT_CHUNKS):
        parts = partials(ids, mixed, out_own[c], out_other[c], count)
        pieces.append(
            [parts[0]]
            + [permute(parts[k], "tensor", lambda i, k=k: i - k) for k in range(1, count)]
        )
    return leave(rows, pieces)[None]


def shifted(block, axis, distance):
    return permute(block, axis, lambda i: i - distance)


def head_norm_rope(vectors, cosine, signed_sine):
    meansq = jnp.mean(vectors * vectors, axis=-1, keepdims=True)
    normed = vectors * lax.rsqrt(meansq + EPSILON)
    return normed * cosine + jnp.roll(normed, vectors.shape[-1] // 2, axis=-1) * signed_sine


def rebuilt(weights):
    before = shifted(weights, "section", 1).astype(jnp.float32)
    after = shifted(weights, "section", -1).astype(jnp.float32)
    return (BEFORE_SHARE * before + AFTER_SHARE * after).astype(jnp.bfloat16)


def general_body(entering, w_query, w_keyval, w_out):
    rows = entering[0].astype(jnp.float32)
    features = rows.shape[1] * lax.axis_size("tensor")
    square_total = lax.psum(jnp.sum(rows * rows, axis=-1, keepdims=True), "tensor")
    normed = (rows * lax.rsqrt(square_total / features + EPSILON)).astype(jnp.bfloat16)
    normed = lax.all_gather(normed, "tensor", axis=1, tiled=True)
    length = normed.shape[0]
    query_weight = lax.all_gather(rebuilt(w_query)[0], "fsdp", axis=0, tiled=True)
    keyval_weight = lax.all_gather(rebuilt(w_keyval)[0], "fsdp", axis=0, tiled=True)
    out_weight = lax.all_gather(rebuilt(w_out)[0], "fsdp", axis=1, tiled=True)
    kv_count = keyval_weight.shape[1]
    raw = jnp.dot(normed, query_weight, preferred_element_type=jnp.float32)
    raw = raw.reshape(length, kv_count, -1, HEAD_DIM)
    keyval_raw = jnp.dot(
        normed, keyval_weight.reshape(features, -1), preferred_element_type=jnp.float32
    ).reshape(length, kv_count, 2 * HEAD_DIM)
    cosine, sine = rope_tables(length, HEAD_DIM)
    queries = head_norm_rope(raw, cosine[:, None, None], sine[:, None, None]).astype(jnp.bfloat16)
    keys = head_norm_rope(
        keyval_raw[..., :HEAD_DIM], cosine[:, None], sine[:, None]
    ).astype(jnp.bfloat16)
    values = keyval_raw[..., HEAD_DIM:].astype(jnp.bfloat16)
    causal = jnp.arange(length)[:, None] >= jnp.arange(length)[None, :]

    def one_group(query_slice):
        scores = jnp.einsum("qkd,pkd->kqp", query_slice, keys, preferred_element_type=jnp.float32)
        expo = jnp.exp(scores * (1.0 / math.sqrt(HEAD_DIM)) - math.sqrt(HEAD_DIM))
        expo = jnp.where(causal[None], expo, 0.0)
        weights = (expo / jnp.sum(expo, axis=-1, keepdims=True)).astype(jnp.bfloat16)
        return jnp.einsum(
            "kqp,pkd->qkd", weights, values, preferred_element_type=jnp.float32
        ).astype(jnp.bfloat16)

    mixed = lax.map(one_group, jnp.moveaxis(queries, 2, 0))
    mixed = jnp.moveaxis(mixed, 0, 2).reshape(length, -1)
    terms = jnp.dot(mixed, out_weight, preferred_element_type=jnp.float32).astype(jnp.bfloat16)
    summed = lax.psum_scatter(terms, "tensor", scatter_dimension=1, tiled=True)
    return (rows + summed.astype(jnp.float32)).astype(jnp.bfloat16)[None]


def solution(mesh):
    in_specs = (
        P("section", "fsdp", "tensor"),
        P("section", "fsdp", "tensor"),
        P("section", "fsdp", "tensor", None),
        P("section", "tensor", "fsdp"),
    )
    out_specs = P("section", "fsdp", "tensor")

    def step(entering, w_query, w_keyval, w_out):
        chunked = (
            mesh.shape["section"] % 2 == 0
            and mesh.shape["fsdp"] == 2
            and mesh.shape["tensor"] % 2 == 0
            and w_keyval.shape[2] == mesh.shape["tensor"]
            and w_keyval.shape[3] == 2 * HEAD_DIM
            and w_query.shape[2] % (mesh.shape["tensor"] * QUERY_CHUNKS * HEAD_DIM) == 0
            and w_out.shape[2] % (mesh.shape["tensor"] * OUT_CHUNKS * LANES) == 0
        )
        return jax.shard_map(
            body if chunked else general_body,
            mesh=mesh,
            in_specs=in_specs,
            out_specs=out_specs,
            check_vma=False,
        )(entering, w_query, w_keyval, w_out)

    return step
```

```python
import functools
import math

import jax
import jax.numpy as jnp
from jax import lax
from jax.experimental import pallas as pl
from jax.experimental.pallas import tpu as pltpu
from jax.sharding import PartitionSpec as P

HEAD_DIM = 128
EPSILON = 1e-06
ROPE_BASE = 1000000.0
BEFORE_SHARE = 0.6
AFTER_SHARE = 0.4
LANES = 128
VMEM_BYTES = 48 * 1024 * 1024
QUERY_CHUNKS = 4
OUT_CHUNKS = 4

SMEM = pl.BlockSpec(memory_space=pltpu.SMEM)
VMEM = pl.BlockSpec(memory_space=pltpu.VMEM)


def params():
    return pltpu.CompilerParams(vmem_limit_bytes=VMEM_BYTES)


def rope_tables(length, width):
    half_width = width // 2
    exponent = jnp.arange(half_width, dtype=jnp.float32) * (2.0 / width)
    inverse = jnp.exp(-exponent * math.log(ROPE_BASE))
    angles = jnp.arange(length, dtype=jnp.float32)[:, None] * inverse[None, :]
    cosine, sine = jnp.cos(angles), jnp.sin(angles)
    return jnp.concatenate([cosine, cosine], axis=1), jnp.concatenate([-sine, sine], axis=1)


ANY = pl.BlockSpec(memory_space=pl.ANY)


def combine_kernel(shares, near, far, *rest):
    out = rest[-1]
    mixed = shares[0] * near[...].astype(jnp.float32) + shares[1] * far[...].astype(jnp.float32)
    out[...] = mixed.astype(out.dtype)


def combine(shares, near, far, after=()):
    rows, columns = far.shape
    step = min(rows, 512)
    block = pl.BlockSpec((step, columns), lambda i: (i, 0))
    return pl.pallas_call(
        combine_kernel,
        out_shape=jax.ShapeDtypeStruct(far.shape, far.dtype),
        grid=(rows // step,),
        in_specs=[SMEM, block, block] + [ANY] * len(after),
        out_specs=block,
        compiler_params=params(),
        cost_estimate=pl.CostEstimate(
            flops=3 * far.size, bytes_accessed=6 * far.size, transcendentals=0
        ),
    )(shares, near, far, *after)


def project(ids, blocks, own, other, whole):
    half = own.shape[0]
    mine, place, count = ids[0], ids[1], len(blocks)
    whole[pl.ds(pl.multiple_of(mine * half, half), half), :] = own[...]
    whole[pl.ds(pl.multiple_of((1 - mine) * half, half), half), :] = other[...]
    total = None
    for k, block in enumerate(blocks):
        width = block.shape[1]
        owner = lax.rem(place - k + count, count)
        rows = pl.ds(pl.multiple_of(owner * width, width), width)
        term = jnp.dot(block[...], whole[rows, :], preferred_element_type=jnp.float32)
        total = term if total is None else total + term
    return total


def norm_rope(vectors, cosine, signed_sine):
    meansq = jnp.mean(vectors * vectors, axis=-1, keepdims=True)
    normed = vectors * lax.rsqrt(meansq + EPSILON)
    return normed * cosine + pltpu.roll(normed, HEAD_DIM // 2, 1) * signed_sine


def keyval_kernel(count, ids, *refs):
    blocks = refs[:count]
    own, other, cosine, sine = refs[count : count + 4]
    keys, values, scales, whole = refs[-4:]
    total = 0.0
    features = 0
    for block in blocks:
        rows = block[...].astype(jnp.float32)
        total = total + jnp.sum(rows * rows, axis=-1, keepdims=True)
        features += block.shape[1]
    scale = lax.rsqrt(total / features + EPSILON)
    raw = project(ids, blocks, own, other, whole) * scale
    keys[...] = norm_rope(raw[:, :HEAD_DIM], cosine[...], sine[...]).astype(keys.dtype)
    values[...] = raw[:, HEAD_DIM:].astype(values.dtype)
    scales[...] = jnp.broadcast_to(scale, scales.shape)


def keyval(ids, blocks, own, other, cosine, sine, after=()):
    length = blocks[0].shape[0]
    features = sum(b.shape[1] for b in blocks)
    head = jax.ShapeDtypeStruct((length, HEAD_DIM), jnp.bfloat16)
    return pl.pallas_call(
        functools.partial(keyval_kernel, len(blocks)),
        out_shape=(head, head, jax.ShapeDtypeStruct((length, LANES), jnp.float32)),
        in_specs=[SMEM] + [VMEM] * (len(blocks) + 4) + [ANY] * len(after),
        out_specs=(VMEM,) * 3,
        scratch_shapes=[pltpu.VMEM((features, own.shape[1]), own.dtype)],
        compiler_params=params(),
        cost_estimate=pl.CostEstimate(
            flops=2 * length * features * own.shape[1],
            bytes_accessed=2 * features * (length + own.shape[1]),
            transcendentals=0,
        ),
    )(ids, *blocks, own, other, cosine, sine, *after)


def attend_kernel(count, ids, *refs):
    blocks = refs[:count]
    own, other, keys, values, scales, cosine, sine = refs[count : count + 7]
    mixed, whole = refs[-2:]
    raw = project(ids, blocks, own, other, whole)
    length = raw.shape[0]
    rows = length // 2 if length % 16 == 0 else length
    scale = scales[:, :1]
    for head in range(raw.shape[1] // HEAD_DIM):
        columns = slice(head * HEAD_DIM, (head + 1) * HEAD_DIM)
        query = norm_rope(raw[:, columns] * scale, cosine[...], sine[...]).astype(jnp.bfloat16)
        for first in range(0, length, rows):
            last = first + rows
            scores = lax.dot_general(
                query[first:last],
                keys[:last, :],
                (((1,), (1,)), ((), ())),
                preferred_element_type=jnp.float32,
            )
            expo = jnp.exp(scores * (1.0 / math.sqrt(HEAD_DIM)) - math.sqrt(HEAD_DIM))
            at = first + lax.broadcasted_iota(jnp.int32, expo.shape, 0)
            expo = jnp.where(lax.broadcasted_iota(jnp.int32, expo.shape, 1) <= at, expo, 0.0)
            total = jnp.sum(expo, axis=-1, keepdims=True)
            product = jnp.dot(
                expo.astype(jnp.bfloat16), values[:last, :], preferred_element_type=jnp.float32
            )
            mixed[first:last, columns] = (product / total).astype(mixed.dtype)


def attend(ids, blocks, own, other, keys, values, scales, cosine, sine, after=()):
    length = blocks[0].shape[0]
    features = sum(b.shape[1] for b in blocks)
    width = own.shape[1]
    return pl.pallas_call(
        functools.partial(attend_kernel, len(blocks)),
        out_shape=jax.ShapeDtypeStruct((length, width), jnp.bfloat16),
        in_specs=[SMEM] + [VMEM] * (len(blocks) + 7) + [ANY] * len(after),
        out_specs=VMEM,
        scratch_shapes=[pltpu.VMEM((features, width), own.dtype)],
        compiler_params=params(),
        cost_estimate=pl.CostEstimate(
            flops=2 * length * features * width + 3 * length * length * width,
            bytes_accessed=2 * features * (length + width),
            transcendentals=length * length * width // HEAD_DIM,
        ),
    )(ids, *blocks, own, other, keys, values, scales, cosine, sine, *after)


def partial_kernel(count, parts, ids, *refs):
    mixed = refs[:parts]
    own, other = refs[parts : parts + 2]
    outs = refs[-1 - count : -1]
    by_owner = refs[-1]
    mine, place = ids[0], ids[1]
    width = by_owner.shape[2]
    per_half = count // 2
    for half, weights in ((mine, own), (1 - mine, other)):
        total = None
        depth = 0
        for part in mixed:
            rows = slice(depth, depth + part.shape[1])
            depth += part.shape[1]
            term = jnp.dot(part[...], weights[rows, :], preferred_element_type=jnp.float32)
            total = term if total is None else total + term
        for piece in range(per_half):
            by_owner[half * per_half + piece] = total[
                :, piece * width : (piece + 1) * width
            ].astype(by_owner.dtype)
    for k in range(count):
        outs[k][...] = by_owner[lax.rem(place + k, count)]


def partials(ids, mixed, own, other, count, after=()):
    length = mixed[0].shape[0]
    width = 2 * own.shape[1] // count
    piece = jax.ShapeDtypeStruct((length, width), jnp.bfloat16)
    return pl.pallas_call(
        functools.partial(partial_kernel, count, len(mixed)),
        out_shape=(piece,) * count,
        in_specs=[SMEM] + [VMEM] * (len(mixed) + 2) + [ANY] * len(after),
        out_specs=(VMEM,) * count,
        scratch_shapes=[pltpu.VMEM((count, length, width), jnp.bfloat16)],
        compiler_params=params(),
        cost_estimate=pl.CostEstimate(
            flops=4 * length * own.size,
            bytes_accessed=4 * own.size + 2 * length * (own.shape[0] + 2 * own.shape[1]),
            transcendentals=0,
        ),
    )(ids, *mixed, own, other, *after)


def leave_kernel(count, chunks, rows, *refs):
    out = refs[-1]
    width = refs[0].shape[1]
    for chunk in range(chunks):
        columns = slice(chunk * width, (chunk + 1) * width)
        pieces = refs[chunk * count : (chunk + 1) * count]
        total = pieces[0][...].astype(jnp.float32)
        for piece in pieces[1:]:
            total = total + piece[...].astype(jnp.float32)
        out[:, columns] = (rows[:, columns].astype(jnp.float32) + total).astype(out.dtype)


def leave(rows, pieces):
    flat = [piece for chunk in pieces for piece in chunk]
    return pl.pallas_call(
        functools.partial(leave_kernel, len(pieces[0]), len(pieces)),
        out_shape=jax.ShapeDtypeStruct(rows.shape, rows.dtype),
        in_specs=[VMEM] * (1 + len(flat)),
        out_specs=VMEM,
        compiler_params=params(),
        cost_estimate=pl.CostEstimate(
            flops=(1 + len(pieces[0])) * rows.size,
            bytes_accessed=2 * rows.size * (2 + len(pieces[0])),
            transcendentals=0,
        ),
    )(rows, *flat)


def permute(array, axis, source):
    count = lax.axis_size(axis)
    return lax.ppermute(array, axis, [(source(i) % count, i) for i in range(count)])


def from_near(array):
    return permute(array, "section", lambda i: i ^ 1)


def from_far(array):
    return permute(array, "section", lambda i: i + 1 if i % 2 else i - 1)


def from_other_half(array):
    return permute(array, "fsdp", lambda i: i ^ 1)


def body(entering, w_query, w_keyval, w_out):
    count = lax.axis_size("tensor")
    section = lax.axis_index("section")
    ids = jnp.stack([lax.axis_index("fsdp"), lax.axis_index("tensor")]).astype(jnp.int32)
    shares = jnp.where(
        section % 2 == 0,
        jnp.array([AFTER_SHARE, BEFORE_SHARE], jnp.float32),
        jnp.array([BEFORE_SHARE, AFTER_SHARE], jnp.float32),
    )
    rows = entering[0]
    length = rows.shape[0]
    own_query = w_query[0]
    own_keyval = w_keyval.reshape(w_keyval.shape[1], -1)
    own_out = w_out[0]
    query_width = own_query.shape[1] // QUERY_CHUNKS
    halves = count // 2
    quarter = own_out.shape[1] // halves
    out_width = quarter // OUT_CHUNKS

    chunks = [own_keyval]
    for c in range(QUERY_CHUNKS):
        chunks.append(own_query[:, c * query_width : (c + 1) * query_width])
    for c in range(OUT_CHUNKS):
        columns = [
            own_out[:, h * quarter + c * out_width : h * quarter + (c + 1) * out_width]
            for h in range(halves)
        ]
        chunks.append(jnp.concatenate(columns, axis=1))
    far = [from_far(chunk) for chunk in chunks]
    near = [from_near(chunk) for chunk in chunks]
    blocks = [rows] + [permute(rows, "tensor", lambda i, k=k: i - k) for k in range(1, count)]
    cosine, sine = rope_tables(length, HEAD_DIM)

    own, other, mixed, pieces = [], [], [], []
    after = {1: blocks[1:2] + blocks[3:], 3: blocks[2:3]}
    for c in range(len(chunks)):
        ready = after.get(c, [])
        if c >= 2:
            ready = ready + [other[c - 2]]
        own.append(combine(shares, near[c], far[c], after=ready))
        other.append(from_other_half(own[c]))
        work = after.setdefault(c + 1, [])
        todo = {3: (0, 1), 4: (2, 3), 5: (4,), 6: (5,), 7: (6,), 8: (7, 8)}.get(c, ())
        for d in todo:
            if d == 0:
                keys, values, scales = keyval(
                    ids, blocks, own[d], other[d], cosine, sine, after=[own[c]]
                )
                work.append(scales)
            elif d <= QUERY_CHUNKS:
                mixed.append(
                    attend(
                        ids,
                        blocks,
                        own[d],
                        other[d],
                        keys,
                        values,
                        scales,
                        cosine,
                        sine,
                        after=[own[c]],
                    )
                )
                work.append(mixed[-1])
            else:
                before = [own[c]] + (pieces[-2][1:] if len(pieces) >= 2 else [])
                parts = partials(ids, mixed, own[d], other[d], count, after=before)
                pieces.append(
                    [parts[0]]
                    + [permute(parts[k], "tensor", lambda i, k=k: i - k) for k in range(1, count)]
                )
                work.append(parts[0])
                after.setdefault(c + 2, []).extend(pieces[-1][1:])
    return leave(rows, pieces)[None]


def shifted(block, axis, distance):
    return permute(block, axis, lambda i: i - distance)


def head_norm_rope(vectors, cosine, signed_sine):
    meansq = jnp.mean(vectors * vectors, axis=-1, keepdims=True)
    normed = vectors * lax.rsqrt(meansq + EPSILON)
    return normed * cosine + jnp.roll(normed, vectors.shape[-1] // 2, axis=-1) * signed_sine


def rebuilt(weights):
    before = shifted(weights, "section", 1).astype(jnp.float32)
    after = shifted(weights, "section", -1).astype(jnp.float32)
    return (BEFORE_SHARE * before + AFTER_SHARE * after).astype(jnp.bfloat16)


def general_body(entering, w_query, w_keyval, w_out):
    rows = entering[0].astype(jnp.float32)
    features = rows.shape[1] * lax.axis_size("tensor")
    square_total = lax.psum(jnp.sum(rows * rows, axis=-1, keepdims=True), "tensor")
    normed = (rows * lax.rsqrt(square_total / features + EPSILON)).astype(jnp.bfloat16)
    normed = lax.all_gather(normed, "tensor", axis=1, tiled=True)
    length = normed.shape[0]
    query_weight = lax.all_gather(rebuilt(w_query)[0], "fsdp", axis=0, tiled=True)
    keyval_weight = lax.all_gather(rebuilt(w_keyval)[0], "fsdp", axis=0, tiled=True)
    out_weight = lax.all_gather(rebuilt(w_out)[0], "fsdp", axis=1, tiled=True)
    kv_count = keyval_weight.shape[1]
    raw = jnp.dot(normed, query_weight, preferred_element_type=jnp.float32)
    raw = raw.reshape(length, kv_count, -1, HEAD_DIM)
    keyval_raw = jnp.dot(
        normed, keyval_weight.reshape(features, -1), preferred_element_type=jnp.float32
    ).reshape(length, kv_count, 2 * HEAD_DIM)
    cosine, sine = rope_tables(length, HEAD_DIM)
    queries = head_norm_rope(raw, cosine[:, None, None], sine[:, None, None]).astype(jnp.bfloat16)
    keys = head_norm_rope(
        keyval_raw[..., :HEAD_DIM], cosine[:, None], sine[:, None]
    ).astype(jnp.bfloat16)
    values = keyval_raw[..., HEAD_DIM:].astype(jnp.bfloat16)
    causal = jnp.arange(length)[:, None] >= jnp.arange(length)[None, :]

    def one_group(query_slice):
        scores = jnp.einsum("qkd,pkd->kqp", query_slice, keys, preferred_element_type=jnp.float32)
        expo = jnp.exp(scores * (1.0 / math.sqrt(HEAD_DIM)) - math.sqrt(HEAD_DIM))
        expo = jnp.where(causal[None], expo, 0.0)
        weights = (expo / jnp.sum(expo, axis=-1, keepdims=True)).astype(jnp.bfloat16)
        return jnp.einsum(
            "kqp,pkd->qkd", weights, values, preferred_element_type=jnp.float32
        ).astype(jnp.bfloat16)

    mixed = lax.map(one_group, jnp.moveaxis(queries, 2, 0))
    mixed = jnp.moveaxis(mixed, 0, 2).reshape(length, -1)
    terms = jnp.dot(mixed, out_weight, preferred_element_type=jnp.float32).astype(jnp.bfloat16)
    summed = lax.psum_scatter(terms, "tensor", scatter_dimension=1, tiled=True)
    return (rows + summed.astype(jnp.float32)).astype(jnp.bfloat16)[None]


def solution(mesh):
    in_specs = (
        P("section", "fsdp", "tensor"),
        P("section", "fsdp", "tensor"),
        P("section", "fsdp", "tensor", None),
        P("section", "tensor", "fsdp"),
    )
    out_specs = P("section", "fsdp", "tensor")

    def step(entering, w_query, w_keyval, w_out):
        chunked = (
            mesh.shape["section"] % 2 == 0
            and mesh.shape["fsdp"] == 2
            and mesh.shape["tensor"] % 2 == 0
            and w_keyval.shape[2] == mesh.shape["tensor"]
            and w_keyval.shape[3] == 2 * HEAD_DIM
            and w_query.shape[2] % (mesh.shape["tensor"] * QUERY_CHUNKS * HEAD_DIM) == 0
            and w_out.shape[2] % (mesh.shape["tensor"] * OUT_CHUNKS * LANES) == 0
        )
        return jax.shard_map(
            body if chunked else general_body,
            mesh=mesh,
            in_specs=in_specs,
            out_specs=out_specs,
            check_vma=False,
        )(entering, w_query, w_keyval, w_out)

    return step
```

```python
import functools
import math

import jax
import jax.numpy as jnp
from jax import lax
from jax.experimental import pallas as pl
from jax.experimental.pallas import tpu as pltpu
from jax.sharding import PartitionSpec as P

HEAD_DIM = 128
EPSILON = 1e-06
ROPE_BASE = 1000000.0
BEFORE_SHARE = 0.6
AFTER_SHARE = 0.4
LANES = 128
VMEM_BYTES = 48 * 1024 * 1024
QUERY_CHUNKS = 4
OUT_CHUNKS = 4
DEPTH = 2
COST = 1
FIRST = (1, 3)
A2A = False
TODO = {3: (0, 1), 4: (2, 3), 5: (4,), 6: (5,), 7: (6,), 8: (7, 8)}
Z_TIE = 2

SMEM = pl.BlockSpec(memory_space=pltpu.SMEM)
VMEM = pl.BlockSpec(memory_space=pltpu.VMEM)


def params():
    return pltpu.CompilerParams(vmem_limit_bytes=VMEM_BYTES)


def rope_tables(length, width):
    half_width = width // 2
    exponent = jnp.arange(half_width, dtype=jnp.float32) * (2.0 / width)
    inverse = jnp.exp(-exponent * math.log(ROPE_BASE))
    angles = jnp.arange(length, dtype=jnp.float32)[:, None] * inverse[None, :]
    cosine, sine = jnp.cos(angles), jnp.sin(angles)
    return jnp.concatenate([cosine, cosine], axis=1), jnp.concatenate([-sine, sine], axis=1)


ANY = pl.BlockSpec(memory_space=pl.ANY)


def combine_kernel(shares, near, far, *rest):
    out = rest[-1]
    mixed = shares[0] * near[...].astype(jnp.float32) + shares[1] * far[...].astype(jnp.float32)
    out[...] = mixed.astype(out.dtype)


def combine(shares, near, far, after=()):
    rows, columns = far.shape
    step = min(rows, 512)
    block = pl.BlockSpec((step, columns), lambda i: (i, 0))
    return pl.pallas_call(
        combine_kernel,
        out_shape=jax.ShapeDtypeStruct(far.shape, far.dtype),
        grid=(rows // step,),
        in_specs=[SMEM, block, block] + [ANY] * len(after),
        out_specs=block,
        compiler_params=params(),
        cost_estimate=pl.CostEstimate(
            flops=3 * far.size, bytes_accessed=COST * 6 * far.size, transcendentals=0
        ),
    )(shares, near, far, *after)


def copy_kernel(source, *rest):
    rest[-1][...] = source[...]


def copied(array, after):
    return pl.pallas_call(
        copy_kernel,
        out_shape=jax.ShapeDtypeStruct(array.shape, array.dtype),
        in_specs=[VMEM] + [ANY] * len(after),
        out_specs=VMEM,
        compiler_params=params(),
        cost_estimate=pl.CostEstimate(flops=0, bytes_accessed=4 * array.size, transcendentals=0),
    )(array, *after)


def project(ids, blocks, own, other, whole):
    half = own.shape[0]
    mine, place, count = ids[0], ids[1], len(blocks)
    whole[pl.ds(pl.multiple_of(mine * half, half), half), :] = own[...]
    whole[pl.ds(pl.multiple_of((1 - mine) * half, half), half), :] = other[...]
    total = None
    for k, block in enumerate(blocks):
        width = block.shape[1]
        owner = lax.rem(place - k + count, count)
        rows = pl.ds(pl.multiple_of(owner * width, width), width)
        term = jnp.dot(block[...], whole[rows, :], preferred_element_type=jnp.float32)
        total = term if total is None else total + term
    return total


def norm_rope(vectors, cosine, signed_sine):
    meansq = jnp.mean(vectors * vectors, axis=-1, keepdims=True)
    normed = vectors * lax.rsqrt(meansq + EPSILON)
    return normed * cosine + pltpu.roll(normed, HEAD_DIM // 2, 1) * signed_sine


def keyval_kernel(count, ids, *refs):
    blocks = refs[:count]
    own, other, cosine, sine = refs[count : count + 4]
    keys, values, scales, whole = refs[-4:]
    total = 0.0
    features = 0
    for block in blocks:
        rows = block[...].astype(jnp.float32)
        total = total + jnp.sum(rows * rows, axis=-1, keepdims=True)
        features += block.shape[1]
    scale = lax.rsqrt(total / features + EPSILON)
    raw = project(ids, blocks, own, other, whole) * scale
    keys[...] = norm_rope(raw[:, :HEAD_DIM], cosine[...], sine[...]).astype(keys.dtype)
    values[...] = raw[:, HEAD_DIM:].astype(values.dtype)
    scales[...] = jnp.broadcast_to(scale, scales.shape)


def keyval(ids, blocks, own, other, cosine, sine, after=()):
    length = blocks[0].shape[0]
    features = sum(b.shape[1] for b in blocks)
    head = jax.ShapeDtypeStruct((length, HEAD_DIM), jnp.bfloat16)
    return pl.pallas_call(
        functools.partial(keyval_kernel, len(blocks)),
        out_shape=(head, head, jax.ShapeDtypeStruct((length, LANES), jnp.float32)),
        in_specs=[SMEM] + [VMEM] * (len(blocks) + 4) + [ANY] * len(after),
        out_specs=(VMEM,) * 3,
        scratch_shapes=[pltpu.VMEM((features, own.shape[1]), own.dtype)],
        compiler_params=params(),
        cost_estimate=pl.CostEstimate(
            flops=2 * length * features * own.shape[1],
            bytes_accessed=2 * features * (length + own.shape[1]),
            transcendentals=0,
        ),
    )(ids, *blocks, own, other, cosine, sine, *after)


def attend_kernel(count, ids, *refs):
    blocks = refs[:count]
    own, other, keys, values, scales, cosine, sine = refs[count : count + 7]
    mixed, whole = refs[-2:]
    raw = project(ids, blocks, own, other, whole)
    length = raw.shape[0]
    rows = length // 2 if length % 16 == 0 else length
    scale = scales[:, :1]
    for head in range(raw.shape[1] // HEAD_DIM):
        columns = slice(head * HEAD_DIM, (head + 1) * HEAD_DIM)
        query = norm_rope(raw[:, columns] * scale, cosine[...], sine[...]).astype(jnp.bfloat16)
        for first in range(0, length, rows):
            last = first + rows
            scores = lax.dot_general(
                query[first:last],
                keys[:last, :],
                (((1,), (1,)), ((), ())),
                preferred_element_type=jnp.float32,
            )
            expo = jnp.exp(scores * (1.0 / math.sqrt(HEAD_DIM)) - math.sqrt(HEAD_DIM))
            at = first + lax.broadcasted_iota(jnp.int32, expo.shape, 0)
            expo = jnp.where(lax.broadcasted_iota(jnp.int32, expo.shape, 1) <= at, expo, 0.0)
            total = jnp.sum(expo, axis=-1, keepdims=True)
            product = jnp.dot(
                expo.astype(jnp.bfloat16), values[:last, :], preferred_element_type=jnp.float32
            )
            mixed[first:last, columns] = (product / total).astype(mixed.dtype)


def attend(ids, blocks, own, other, keys, values, scales, cosine, sine, after=()):
    length = blocks[0].shape[0]
    features = sum(b.shape[1] for b in blocks)
    width = own.shape[1]
    return pl.pallas_call(
        functools.partial(attend_kernel, len(blocks)),
        out_shape=jax.ShapeDtypeStruct((length, width), jnp.bfloat16),
        in_specs=[SMEM] + [VMEM] * (len(blocks) + 7) + [ANY] * len(after),
        out_specs=VMEM,
        scratch_shapes=[pltpu.VMEM((features, width), own.dtype)],
        compiler_params=params(),
        cost_estimate=pl.CostEstimate(
            flops=2 * length * features * width + 3 * length * length * width,
            bytes_accessed=2 * features * (length + width),
            transcendentals=length * length * width // HEAD_DIM,
        ),
    )(ids, *blocks, own, other, keys, values, scales, cosine, sine, *after)


def partial_kernel(count, parts, ids, *refs):
    mixed = refs[:parts]
    own, other = refs[parts : parts + 2]
    if A2A:
        by_owner = refs[-1]
    else:
        outs = refs[-1 - count : -1]
        by_owner = refs[-1]
    mine, place = ids[0], ids[1]
    width = by_owner.shape[2]
    per_half = count // 2
    for half, weights in ((mine, own), (1 - mine, other)):
        total = None
        depth = 0
        for part in mixed:
            rows = slice(depth, depth + part.shape[1])
            depth += part.shape[1]
            term = jnp.dot(part[...], weights[rows, :], preferred_element_type=jnp.float32)
            total = term if total is None else total + term
        for piece in range(per_half):
            by_owner[half * per_half + piece] = total[
                :, piece * width : (piece + 1) * width
            ].astype(by_owner.dtype)
    if not A2A:
        for k in range(count):
            outs[k][...] = by_owner[lax.rem(place + k, count)]


def partials(ids, mixed, own, other, count, after=()):
    length = mixed[0].shape[0]
    width = 2 * own.shape[1] // count
    piece = jax.ShapeDtypeStruct((length, width), jnp.bfloat16)
    return pl.pallas_call(
        functools.partial(partial_kernel, count, len(mixed)),
        out_shape=jax.ShapeDtypeStruct((count, length, width), jnp.bfloat16) if A2A else (piece,) * count,
        in_specs=[SMEM] + [VMEM] * (len(mixed) + 2) + [ANY] * len(after),
        out_specs=VMEM if A2A else (VMEM,) * count,
        scratch_shapes=[] if A2A else [pltpu.VMEM((count, length, width), jnp.bfloat16)],
        compiler_params=params(),
        cost_estimate=pl.CostEstimate(
            flops=4 * length * own.size,
            bytes_accessed=4 * own.size + 2 * length * (own.shape[0] + 2 * own.shape[1]),
            transcendentals=0,
        ),
    )(ids, *mixed, own, other, *after)


def leave_kernel(chunks, rows, *refs):
    out = refs[-1]
    per_chunk = (len(refs) - 1) // chunks
    width = rows.shape[1] // chunks
    for chunk in range(chunks):
        columns = slice(chunk * width, (chunk + 1) * width)
        total = None
        for piece in refs[chunk * per_chunk : (chunk + 1) * per_chunk]:
            term = piece[...].astype(jnp.float32)
            term = jnp.sum(term, axis=0) if len(piece.shape) == 3 else term
            total = term if total is None else total + term
        out[:, columns] = (rows[:, columns].astype(jnp.float32) + total).astype(out.dtype)


def leave(rows, pieces):
    flat = [piece for chunk in pieces for piece in chunk]
    return pl.pallas_call(
        functools.partial(leave_kernel, len(pieces)),
        out_shape=jax.ShapeDtypeStruct(rows.shape, rows.dtype),
        in_specs=[VMEM] * (1 + len(flat)),
        out_specs=VMEM,
        compiler_params=params(),
        cost_estimate=pl.CostEstimate(
            flops=5 * rows.size, bytes_accessed=12 * rows.size, transcendentals=0
        ),
    )(rows, *flat)


def permute(array, axis, source):
    count = lax.axis_size(axis)
    return lax.ppermute(array, axis, [(source(i) % count, i) for i in range(count)])


def from_near(array):
    return permute(array, "section", lambda i: i ^ 1)


def from_far(array):
    return permute(array, "section", lambda i: i + 1 if i % 2 else i - 1)


def from_other_half(array):
    return permute(array, "fsdp", lambda i: i ^ 1)


def body(entering, w_query, w_keyval, w_out):
    count = lax.axis_size("tensor")
    section = lax.axis_index("section")
    ids = jnp.stack([lax.axis_index("fsdp"), lax.axis_index("tensor")]).astype(jnp.int32)
    shares = jnp.where(
        section % 2 == 0,
        jnp.array([AFTER_SHARE, BEFORE_SHARE], jnp.float32),
        jnp.array([BEFORE_SHARE, AFTER_SHARE], jnp.float32),
    )
    rows = entering[0]
    length = rows.shape[0]
    own_query = w_query[0]
    own_keyval = w_keyval.reshape(w_keyval.shape[1], -1)
    own_out = w_out[0]
    query_width = own_query.shape[1] // QUERY_CHUNKS
    halves = count // 2
    quarter = own_out.shape[1] // halves
    out_width = quarter // OUT_CHUNKS

    chunks = [own_keyval]
    for c in range(QUERY_CHUNKS):
        chunks.append(own_query[:, c * query_width : (c + 1) * query_width])
    for c in range(OUT_CHUNKS):
        columns = [
            own_out[:, h * quarter + c * out_width : h * quarter + (c + 1) * out_width]
            for h in range(halves)
        ]
        chunks.append(jnp.concatenate(columns, axis=1))
    far = [from_far(chunk) for chunk in chunks]
    near = [from_near(chunk) for chunk in chunks]
    blocks = [rows] + [None] * (count - 1)
    for k in FIRST:
        blocks[k] = permute(rows, "tensor", lambda i, k=k: i - k)
    again = copied(rows, after=[blocks[k] for k in FIRST])
    for k in range(1, count):
        if k not in FIRST:
            blocks[k] = permute(again, "tensor", lambda i, k=k: i - k)
    cosine, sine = rope_tables(length, HEAD_DIM)

    own, other, mixed, pieces = [], [], [], []
    after = {}
    for c in range(len(chunks)):
        ready = after.get(c, [])
        if c >= DEPTH:
            ready = ready + [other[c - DEPTH]]
        own.append(combine(shares, near[c], far[c], after=ready))
        other.append(from_other_half(own[c]))
        work = after.setdefault(c + 1, [])
        for d in TODO.get(c, ()):
            if d == 0:
                keys, values, scales = keyval(
                    ids, blocks, own[d], other[d], cosine, sine, after=[own[c]]
                )
                work.append(scales)
            elif d <= QUERY_CHUNKS:
                mixed.append(
                    attend(
                        ids,
                        blocks,
                        own[d],
                        other[d],
                        keys,
                        values,
                        scales,
                        cosine,
                        sine,
                        after=[own[c]],
                    )
                )
                work.append(mixed[-1])
            else:
                before = [own[c]] + (pieces[-2][-3:] if len(pieces) >= 2 else [])
                parts = partials(ids, mixed, own[d], other[d], count, after=before)
                if A2A:
                    work.append(parts)
                    pieces.append([lax.all_to_all(parts, "tensor", 0, 0)])
                else:
                    pieces.append(
                        [parts[0]]
                        + [permute(parts[k], "tensor", lambda i, k=k: i - k) for k in range(1, count)]
                    )
                    work.append(parts[0])
                after.setdefault(c + Z_TIE, []).extend(pieces[-1][-3:])
    return leave(rows, pieces)[None]


def shifted(block, axis, distance):
    return permute(block, axis, lambda i: i - distance)


def head_norm_rope(vectors, cosine, signed_sine):
    meansq = jnp.mean(vectors * vectors, axis=-1, keepdims=True)
    normed = vectors * lax.rsqrt(meansq + EPSILON)
    return normed * cosine + jnp.roll(normed, vectors.shape[-1] // 2, axis=-1) * signed_sine


def rebuilt(weights):
    before = shifted(weights, "section", 1).astype(jnp.float32)
    after = shifted(weights, "section", -1).astype(jnp.float32)
    return (BEFORE_SHARE * before + AFTER_SHARE * after).astype(jnp.bfloat16)


def general_body(entering, w_query, w_keyval, w_out):
    rows = entering[0].astype(jnp.float32)
    features = rows.shape[1] * lax.axis_size("tensor")
    square_total = lax.psum(jnp.sum(rows * rows, axis=-1, keepdims=True), "tensor")
    normed = (rows * lax.rsqrt(square_total / features + EPSILON)).astype(jnp.bfloat16)
    normed = lax.all_gather(normed, "tensor", axis=1, tiled=True)
    length = normed.shape[0]
    query_weight = lax.all_gather(rebuilt(w_query)[0], "fsdp", axis=0, tiled=True)
    keyval_weight = lax.all_gather(rebuilt(w_keyval)[0], "fsdp", axis=0, tiled=True)
    out_weight = lax.all_gather(rebuilt(w_out)[0], "fsdp", axis=1, tiled=True)
    kv_count = keyval_weight.shape[1]
    raw = jnp.dot(normed, query_weight, preferred_element_type=jnp.float32)
    raw = raw.reshape(length, kv_count, -1, HEAD_DIM)
    keyval_raw = jnp.dot(
        normed, keyval_weight.reshape(features, -1), preferred_element_type=jnp.float32
    ).reshape(length, kv_count, 2 * HEAD_DIM)
    cosine, sine = rope_tables(length, HEAD_DIM)
    queries = head_norm_rope(raw, cosine[:, None, None], sine[:, None, None]).astype(jnp.bfloat16)
    keys = head_norm_rope(
        keyval_raw[..., :HEAD_DIM], cosine[:, None], sine[:, None]
    ).astype(jnp.bfloat16)
    values = keyval_raw[..., HEAD_DIM:].astype(jnp.bfloat16)
    causal = jnp.arange(length)[:, None] >= jnp.arange(length)[None, :]

    def one_group(query_slice):
        scores = jnp.einsum("qkd,pkd->kqp", query_slice, keys, preferred_element_type=jnp.float32)
        expo = jnp.exp(scores * (1.0 / math.sqrt(HEAD_DIM)) - math.sqrt(HEAD_DIM))
        expo = jnp.where(causal[None], expo, 0.0)
        weights = (expo / jnp.sum(expo, axis=-1, keepdims=True)).astype(jnp.bfloat16)
        return jnp.einsum(
            "kqp,pkd->qkd", weights, values, preferred_element_type=jnp.float32
        ).astype(jnp.bfloat16)

    mixed = lax.map(one_group, jnp.moveaxis(queries, 2, 0))
    mixed = jnp.moveaxis(mixed, 0, 2).reshape(length, -1)
    terms = jnp.dot(mixed, out_weight, preferred_element_type=jnp.float32).astype(jnp.bfloat16)
    summed = lax.psum_scatter(terms, "tensor", scatter_dimension=1, tiled=True)
    return (rows + summed.astype(jnp.float32)).astype(jnp.bfloat16)[None]


def solution(mesh):
    in_specs = (
        P("section", "fsdp", "tensor"),
        P("section", "fsdp", "tensor"),
        P("section", "fsdp", "tensor", None),
        P("section", "tensor", "fsdp"),
    )
    out_specs = P("section", "fsdp", "tensor")

    def step(entering, w_query, w_keyval, w_out):
        chunked = (
            mesh.shape["section"] % 2 == 0
            and mesh.shape["fsdp"] == 2
            and mesh.shape["tensor"] % 2 == 0
            and w_keyval.shape[2] == mesh.shape["tensor"]
            and w_keyval.shape[3] == 2 * HEAD_DIM
            and w_query.shape[2] % (mesh.shape["tensor"] * QUERY_CHUNKS * HEAD_DIM) == 0
            and w_out.shape[2] % (mesh.shape["tensor"] * OUT_CHUNKS * LANES) == 0
        )
        return jax.shard_map(
            body if chunked else general_body,
            mesh=mesh,
            in_specs=in_specs,
            out_specs=out_specs,
            check_vma=False,
        )(entering, w_query, w_keyval, w_out)

    return step
```

```python
import functools
import math

import jax
import jax.numpy as jnp
import numpy as np
from jax import lax
from jax.experimental import pallas as pl
from jax.experimental.pallas import tpu as pltpu
from jax.sharding import PartitionSpec as P

HEAD_DIM = 128
EPSILON = 1e-06
ROPE_BASE = 1000000.0
BEFORE_SHARE = 0.6
AFTER_SHARE = 0.4
LANES = 128
VMEM_BYTES = 48 * 1024 * 1024
QUERY_CHUNKS = 4
OUT_CHUNKS = 4
DEPTH = 3
COST = 4000
KEYVAL_COST = 1
ATTEND_COST = 2
PARTIAL_COST = 16
COPY_COST = 16000
AGAIN_TIE = 2
DEPTHS = {1: 1, 2: 2}
COSTS = {}
EXTRA = {3: (2,)}
AGAIN_AFTER = 0
PARTIAL_TIE = 2
NUMPY_TABLES = True
WHOLE_NEAR = False
FIRST = (1, 3)
A2A = False
TODO = {3: (0, 1), 4: (2, 3), 5: (4,), 6: (5,), 7: (6,), 8: (7, 8)}
Z_TIE = 2

SMEM = pl.BlockSpec(memory_space=pltpu.SMEM)
VMEM = pl.BlockSpec(memory_space=pltpu.VMEM)


def params():
    return pltpu.CompilerParams(vmem_limit_bytes=VMEM_BYTES)


def rope_tables(length, width):
    if not NUMPY_TABLES:
        exponent = jnp.arange(width // 2, dtype=jnp.float32) * (2.0 / width)
        angles = jnp.arange(length, dtype=jnp.float32)[:, None] * jnp.exp(
            -exponent * math.log(ROPE_BASE)
        )
        cosine, sine = jnp.cos(angles), jnp.sin(angles)
        return jnp.concatenate([cosine, cosine], 1), jnp.concatenate([-sine, sine], 1)
    inverse = ROPE_BASE ** (np.arange(width // 2) * (-2.0 / width))
    angles = np.arange(length)[:, None] * inverse[None, :]
    cosine, sine = np.cos(angles), np.sin(angles)
    cosine, sine = np.concatenate([cosine, cosine], 1), np.concatenate([-sine, sine], 1)
    return jnp.asarray(cosine, jnp.float32), jnp.asarray(sine, jnp.float32)


ANY = pl.BlockSpec(memory_space=pl.ANY)


def combine_kernel(shares, near, far, *rest):
    out = rest[-1]
    mixed = shares[0] * near[...].astype(jnp.float32) + shares[1] * far[...].astype(jnp.float32)
    out[...] = mixed.astype(out.dtype)


def combine(shares, near, far, after=(), cost=0):
    rows, columns = far.shape
    step = min(rows, 512)
    block = pl.BlockSpec((step, columns), lambda i: (i, 0))
    return pl.pallas_call(
        combine_kernel,
        out_shape=jax.ShapeDtypeStruct(far.shape, far.dtype),
        grid=(rows // step,),
        in_specs=[SMEM, block, block] + [ANY] * len(after),
        out_specs=block,
        compiler_params=params(),
        cost_estimate=pl.CostEstimate(
            flops=cost * far.size, bytes_accessed=6 * far.size, transcendentals=0
        ),
    )(shares, near, far, *after)


def copy_kernel(source, *rest):
    rest[-1][...] = source[...]


def copied(array, after):
    return pl.pallas_call(
        copy_kernel,
        out_shape=jax.ShapeDtypeStruct(array.shape, array.dtype),
        in_specs=[VMEM] + [ANY] * len(after),
        out_specs=VMEM,
        compiler_params=params(),
        cost_estimate=pl.CostEstimate(flops=COPY_COST * array.size, bytes_accessed=4 * array.size, transcendentals=0),
    )(array, *after)


def project(ids, blocks, own, other, whole):
    half = own.shape[0]
    mine, place, count = ids[0], ids[1], len(blocks)
    whole[pl.ds(pl.multiple_of(mine * half, half), half), :] = own[...]
    whole[pl.ds(pl.multiple_of((1 - mine) * half, half), half), :] = other[...]
    total = None
    for k, block in enumerate(blocks):
        width = block.shape[1]
        owner = lax.rem(place - k + count, count)
        rows = pl.ds(pl.multiple_of(owner * width, width), width)
        term = jnp.dot(block[...], whole[rows, :], preferred_element_type=jnp.float32)
        total = term if total is None else total + term
    return total


def norm_rope(vectors, cosine, signed_sine):
    meansq = jnp.mean(vectors * vectors, axis=-1, keepdims=True)
    normed = vectors * lax.rsqrt(meansq + EPSILON)
    return normed * cosine + pltpu.roll(normed, HEAD_DIM // 2, 1) * signed_sine


def keyval_kernel(count, ids, *refs):
    blocks = refs[:count]
    own, other, cosine, sine = refs[count : count + 4]
    keys, values, scales, whole = refs[-4:]
    total = 0.0
    features = 0
    for block in blocks:
        rows = block[...].astype(jnp.float32)
        total = total + jnp.sum(rows * rows, axis=-1, keepdims=True)
        features += block.shape[1]
    scale = lax.rsqrt(total / features + EPSILON)
    raw = project(ids, blocks, own, other, whole) * scale
    keys[...] = norm_rope(raw[:, :HEAD_DIM], cosine[...], sine[...]).astype(keys.dtype)
    values[...] = raw[:, HEAD_DIM:].astype(values.dtype)
    scales[...] = jnp.broadcast_to(scale, scales.shape)


def keyval(ids, blocks, own, other, cosine, sine, after=()):
    length = blocks[0].shape[0]
    features = sum(b.shape[1] for b in blocks)
    head = jax.ShapeDtypeStruct((length, HEAD_DIM), jnp.bfloat16)
    return pl.pallas_call(
        functools.partial(keyval_kernel, len(blocks)),
        out_shape=(head, head, jax.ShapeDtypeStruct((length, LANES), jnp.float32)),
        in_specs=[SMEM] + [VMEM] * (len(blocks) + 4) + [ANY] * len(after),
        out_specs=(VMEM,) * 3,
        scratch_shapes=[pltpu.VMEM((features, own.shape[1]), own.dtype)],
        compiler_params=params(),
        cost_estimate=pl.CostEstimate(
            flops=int(KEYVAL_COST * 2 * length * features * own.shape[1]),
            bytes_accessed=2 * features * (length + own.shape[1]),
            transcendentals=0,
        ),
    )(ids, *blocks, own, other, cosine, sine, *after)


def attend_kernel(count, ids, *refs):
    blocks = refs[:count]
    own, other, keys, values, scales, cosine, sine = refs[count : count + 7]
    mixed, whole = refs[-2:]
    raw = project(ids, blocks, own, other, whole)
    length = raw.shape[0]
    rows = length // 2 if length % 16 == 0 else length
    scale = scales[:, :1]
    for head in range(raw.shape[1] // HEAD_DIM):
        columns = slice(head * HEAD_DIM, (head + 1) * HEAD_DIM)
        query = norm_rope(raw[:, columns] * scale, cosine[...], sine[...]).astype(jnp.bfloat16)
        for first in range(0, length, rows):
            last = first + rows
            scores = lax.dot_general(
                query[first:last],
                keys[:last, :],
                (((1,), (1,)), ((), ())),
                preferred_element_type=jnp.float32,
            )
            expo = jnp.exp(scores * (1.0 / math.sqrt(HEAD_DIM)) - math.sqrt(HEAD_DIM))
            at = first + lax.broadcasted_iota(jnp.int32, expo.shape, 0)
            expo = jnp.where(lax.broadcasted_iota(jnp.int32, expo.shape, 1) <= at, expo, 0.0)
            total = jnp.sum(expo, axis=-1, keepdims=True)
            product = jnp.dot(
                expo.astype(jnp.bfloat16), values[:last, :], preferred_element_type=jnp.float32
            )
            mixed[first:last, columns] = (product / total).astype(mixed.dtype)


def attend(ids, blocks, own, other, keys, values, scales, cosine, sine, after=()):
    length = blocks[0].shape[0]
    features = sum(b.shape[1] for b in blocks)
    width = own.shape[1]
    return pl.pallas_call(
        functools.partial(attend_kernel, len(blocks)),
        out_shape=jax.ShapeDtypeStruct((length, width), jnp.bfloat16),
        in_specs=[SMEM] + [VMEM] * (len(blocks) + 7) + [ANY] * len(after),
        out_specs=VMEM,
        scratch_shapes=[pltpu.VMEM((features, width), own.dtype)],
        compiler_params=params(),
        cost_estimate=pl.CostEstimate(
            flops=int(ATTEND_COST * (2 * length * features * width + 3 * length * length * width)),
            bytes_accessed=2 * features * (length + width),
            transcendentals=length * length * width // HEAD_DIM,
        ),
    )(ids, *blocks, own, other, keys, values, scales, cosine, sine, *after)


def partial_kernel(count, parts, ids, *refs):
    mixed = refs[:parts]
    own, other = refs[parts : parts + 2]
    if A2A:
        by_owner = refs[-1]
    else:
        outs = refs[-1 - count : -1]
        by_owner = refs[-1]
    mine, place = ids[0], ids[1]
    width = by_owner.shape[2]
    per_half = count // 2
    for half, weights in ((mine, own), (1 - mine, other)):
        total = None
        depth = 0
        for part in mixed:
            rows = slice(depth, depth + part.shape[1])
            depth += part.shape[1]
            term = jnp.dot(part[...], weights[rows, :], preferred_element_type=jnp.float32)
            total = term if total is None else total + term
        for piece in range(per_half):
            by_owner[half * per_half + piece] = total[
                :, piece * width : (piece + 1) * width
            ].astype(by_owner.dtype)
    if not A2A:
        for k in range(count):
            outs[k][...] = by_owner[lax.rem(place + k, count)]


def partials(ids, mixed, own, other, count, after=()):
    length = mixed[0].shape[0]
    width = 2 * own.shape[1] // count
    piece = jax.ShapeDtypeStruct((length, width), jnp.bfloat16)
    return pl.pallas_call(
        functools.partial(partial_kernel, count, len(mixed)),
        out_shape=jax.ShapeDtypeStruct((count, length, width), jnp.bfloat16) if A2A else (piece,) * count,
        in_specs=[SMEM] + [VMEM] * (len(mixed) + 2) + [ANY] * len(after),
        out_specs=VMEM if A2A else (VMEM,) * count,
        scratch_shapes=[] if A2A else [pltpu.VMEM((count, length, width), jnp.bfloat16)],
        compiler_params=params(),
        cost_estimate=pl.CostEstimate(
            flops=int(PARTIAL_COST * 4 * length * own.size),
            bytes_accessed=4 * own.size + 2 * length * (own.shape[0] + 2 * own.shape[1]),
            transcendentals=0,
        ),
    )(ids, *mixed, own, other, *after)


def leave_kernel(chunks, rows, *refs):
    out = refs[-1]
    per_chunk = (len(refs) - 1) // chunks
    width = rows.shape[1] // chunks
    for chunk in range(chunks):
        columns = slice(chunk * width, (chunk + 1) * width)
        total = None
        for piece in refs[chunk * per_chunk : (chunk + 1) * per_chunk]:
            term = piece[...].astype(jnp.float32)
            term = jnp.sum(term, axis=0) if len(piece.shape) == 3 else term
            total = term if total is None else total + term
        out[:, columns] = (rows[:, columns].astype(jnp.float32) + total).astype(out.dtype)


def leave(rows, pieces):
    flat = [piece for chunk in pieces for piece in chunk]
    return pl.pallas_call(
        functools.partial(leave_kernel, len(pieces)),
        out_shape=jax.ShapeDtypeStruct(rows.shape, rows.dtype),
        in_specs=[VMEM] * (1 + len(flat)),
        out_specs=VMEM,
        compiler_params=params(),
        cost_estimate=pl.CostEstimate(
            flops=5 * rows.size, bytes_accessed=12 * rows.size, transcendentals=0
        ),
    )(rows, *flat)


def permute(array, axis, source):
    count = lax.axis_size(axis)
    return lax.ppermute(array, axis, [(source(i) % count, i) for i in range(count)])


def from_near(array):
    return permute(array, "section", lambda i: i ^ 1)


def from_far(array):
    return permute(array, "section", lambda i: i + 1 if i % 2 else i - 1)


def from_other_half(array):
    return permute(array, "fsdp", lambda i: i ^ 1)


def body(entering, w_query, w_keyval, w_out):
    count = lax.axis_size("tensor")
    section = lax.axis_index("section")
    ids = jnp.stack([lax.axis_index("fsdp"), lax.axis_index("tensor")]).astype(jnp.int32)
    shares = jnp.where(
        section % 2 == 0,
        jnp.array([AFTER_SHARE, BEFORE_SHARE], jnp.float32),
        jnp.array([BEFORE_SHARE, AFTER_SHARE], jnp.float32),
    )
    rows = entering[0]
    length = rows.shape[0]
    own_query = w_query[0]
    own_keyval = w_keyval.reshape(w_keyval.shape[1], -1)
    own_out = w_out[0]
    query_width = own_query.shape[1] // QUERY_CHUNKS
    halves = count // 2
    quarter = own_out.shape[1] // halves
    out_width = quarter // OUT_CHUNKS

    chunks = [own_keyval]
    for c in range(QUERY_CHUNKS):
        chunks.append(own_query[:, c * query_width : (c + 1) * query_width])
    for c in range(OUT_CHUNKS):
        columns = [
            own_out[:, h * quarter + c * out_width : h * quarter + (c + 1) * out_width]
            for h in range(halves)
        ]
        chunks.append(jnp.concatenate(columns, axis=1))
    far = [from_far(chunk) for chunk in chunks]
    near = [from_near(chunk) for chunk in chunks]
    blocks = [rows] + [None] * (count - 1)
    for k in FIRST:
        blocks[k] = permute(rows, "tensor", lambda i, k=k: i - k)
    first = [blocks[k] for k in FIRST]
    again = copied(rows, after=(first, near[:1], far[:1], near[1:2], first[:1])[AGAIN_AFTER])
    for k in range(1, count):
        if k not in FIRST:
            blocks[k] = permute(again, "tensor", lambda i, k=k: i - k)
    cosine, sine = rope_tables(length, HEAD_DIM)

    own, other, mixed, pieces = [], [], [], []
    after = {AGAIN_TIE: [again]} if AGAIN_TIE else {}
    for c in range(len(chunks)):
        ready = after.get(c, [])
        depth = DEPTHS.get(c, DEPTH)
        if c >= depth:
            ready = ready + [other[c - depth]]
        ready = ready + [other[d] for d in EXTRA.get(c, ()) if d < c]
        own.append(combine(shares, near[c], far[c], after=ready, cost=COSTS.get(c, COST)))
        other.append(from_other_half(own[c]))
        work = after.setdefault(c + 1, [])
        for d in TODO.get(c, ()):
            if d == 0:
                keys, values, scales = keyval(
                    ids, blocks, own[d], other[d], cosine, sine, after=[own[c]]
                )
                work.append(scales)
            elif d <= QUERY_CHUNKS:
                mixed.append(
                    attend(
                        ids,
                        blocks,
                        own[d],
                        other[d],
                        keys,
                        values,
                        scales,
                        cosine,
                        sine,
                        after=[own[c]],
                    )
                )
                work.append(mixed[-1])
            else:
                before = [own[c]] + (pieces[-PARTIAL_TIE][-3:] if len(pieces) >= PARTIAL_TIE else [])
                parts = partials(ids, mixed, own[d], other[d], count, after=before)
                if A2A:
                    work.append(parts)
                    pieces.append([lax.all_to_all(parts, "tensor", 0, 0)])
                else:
                    pieces.append(
                        [parts[0]]
                        + [permute(parts[k], "tensor", lambda i, k=k: i - k) for k in range(1, count)]
                    )
                    work.append(parts[0])
                after.setdefault(c + Z_TIE, []).extend(pieces[-1][-3:])
    return leave(rows, pieces)[None]


def shifted(block, axis, distance):
    return permute(block, axis, lambda i: i - distance)


def head_norm_rope(vectors, cosine, signed_sine):
    meansq = jnp.mean(vectors * vectors, axis=-1, keepdims=True)
    normed = vectors * lax.rsqrt(meansq + EPSILON)
    return normed * cosine + jnp.roll(normed, vectors.shape[-1] // 2, axis=-1) * signed_sine


def rebuilt(weights):
    before = shifted(weights, "section", 1).astype(jnp.float32)
    after = shifted(weights, "section", -1).astype(jnp.float32)
    return (BEFORE_SHARE * before + AFTER_SHARE * after).astype(jnp.bfloat16)


def general_body(entering, w_query, w_keyval, w_out):
    rows = entering[0].astype(jnp.float32)
    features = rows.shape[1] * lax.axis_size("tensor")
    square_total = lax.psum(jnp.sum(rows * rows, axis=-1, keepdims=True), "tensor")
    normed = (rows * lax.rsqrt(square_total / features + EPSILON)).astype(jnp.bfloat16)
    normed = lax.all_gather(normed, "tensor", axis=1, tiled=True)
    length = normed.shape[0]
    query_weight = lax.all_gather(rebuilt(w_query)[0], "fsdp", axis=0, tiled=True)
    keyval_weight = lax.all_gather(rebuilt(w_keyval)[0], "fsdp", axis=0, tiled=True)
    out_weight = lax.all_gather(rebuilt(w_out)[0], "fsdp", axis=1, tiled=True)
    kv_count = keyval_weight.shape[1]
    raw = jnp.dot(normed, query_weight, preferred_element_type=jnp.float32)
    raw = raw.reshape(length, kv_count, -1, HEAD_DIM)
    keyval_raw = jnp.dot(
        normed, keyval_weight.reshape(features, -1), preferred_element_type=jnp.float32
    ).reshape(length, kv_count, 2 * HEAD_DIM)
    cosine, sine = rope_tables(length, HEAD_DIM)
    queries = head_norm_rope(raw, cosine[:, None, None], sine[:, None, None]).astype(jnp.bfloat16)
    keys = head_norm_rope(
        keyval_raw[..., :HEAD_DIM], cosine[:, None], sine[:, None]
    ).astype(jnp.bfloat16)
    values = keyval_raw[..., HEAD_DIM:].astype(jnp.bfloat16)
    causal = jnp.arange(length)[:, None] >= jnp.arange(length)[None, :]

    def one_group(query_slice):
        scores = jnp.einsum("qkd,pkd->kqp", query_slice, keys, preferred_element_type=jnp.float32)
        expo = jnp.exp(scores * (1.0 / math.sqrt(HEAD_DIM)) - math.sqrt(HEAD_DIM))
        expo = jnp.where(causal[None], expo, 0.0)
        weights = (expo / jnp.sum(expo, axis=-1, keepdims=True)).astype(jnp.bfloat16)
        return jnp.einsum(
            "kqp,pkd->qkd", weights, values, preferred_element_type=jnp.float32
        ).astype(jnp.bfloat16)

    mixed = lax.map(one_group, jnp.moveaxis(queries, 2, 0))
    mixed = jnp.moveaxis(mixed, 0, 2).reshape(length, -1)
    terms = jnp.dot(mixed, out_weight, preferred_element_type=jnp.float32).astype(jnp.bfloat16)
    summed = lax.psum_scatter(terms, "tensor", scatter_dimension=1, tiled=True)
    return (rows + summed.astype(jnp.float32)).astype(jnp.bfloat16)[None]


def solution(mesh):
    in_specs = (
        P("section", "fsdp", "tensor"),
        P("section", "fsdp", "tensor"),
        P("section", "fsdp", "tensor", None),
        P("section", "tensor", "fsdp"),
    )
    out_specs = P("section", "fsdp", "tensor")

    def step(entering, w_query, w_keyval, w_out):
        chunked = (
            mesh.shape["section"] % 2 == 0
            and mesh.shape["fsdp"] == 2
            and mesh.shape["tensor"] % 2 == 0
            and w_keyval.shape[2] == mesh.shape["tensor"]
            and w_keyval.shape[3] == 2 * HEAD_DIM
            and w_query.shape[2] % (mesh.shape["tensor"] * QUERY_CHUNKS * HEAD_DIM) == 0
            and w_out.shape[2] % (mesh.shape["tensor"] * OUT_CHUNKS * LANES) == 0
        )
        return jax.shard_map(
            body if chunked else general_body,
            mesh=mesh,
            in_specs=in_specs,
            out_specs=out_specs,
            check_vma=False,
        )(entering, w_query, w_keyval, w_out)

    return step
```

```python
import functools
import math

import jax
import jax.numpy as jnp
import numpy as np
from jax import lax
from jax.experimental import pallas as pl
from jax.experimental.pallas import tpu as pltpu
from jax.sharding import PartitionSpec as P

HEAD_DIM = 128
EPSILON = 1e-06
ROPE_BASE = 1000000.0
BEFORE_SHARE = 0.6
AFTER_SHARE = 0.4
LANES = 128
VMEM_BYTES = 48 * 1024 * 1024
QUERY_CHUNKS = 4
OUT_CHUNKS = 4
FIRST = (1, 3)
STEPS = (('G', 1, '', 200), ('G', 2, 'n0 n1', 200), ('C', 0, '', 1500), ('G', 3, '', 200), ('X', 0, 'a1', 1500), ('C', 1, 'y0', 1500), ('G', 4, '', 200), ('C', 2, '', 1500), ('C', 3, 'y1', 1500), ('G', 5, '', 200), ('G', 6, '', 200), ('K', 0, '', 0), ('A', 1, '', 0), ('C', 4, 'y2', 1500), ('A', 2, '', 6000), ('A', 3, '', 0), ('G', 7, '', 200), ('C', 5, '', 1500), ('G', 8, '', 200), ('A', 4, '', 6000), ('C', 6, '', 1500), ('P', 5, '', 0), ('C', 7, '', 700), ('P', 6, '', 1000), ('R', 5, '', 1000), ('C', 8, '', 1000), ('R', 6, '', 1500), ('Q', 7, '', 200), ('Q', 8, 't5 t6', 0))

SMEM = pl.BlockSpec(memory_space=pltpu.SMEM)
VMEM = pl.BlockSpec(memory_space=pltpu.VMEM)


def estimate(cost):
    return pl.CostEstimate(flops=cost * 2**20, bytes_accessed=0, transcendentals=0)


def params():
    return pltpu.CompilerParams(vmem_limit_bytes=VMEM_BYTES)


def rope_tables(length, width):
    inverse = ROPE_BASE ** (np.arange(width // 2) * (-2.0 / width))
    angles = np.arange(length)[:, None] * inverse[None, :]
    cosine, sine = np.cos(angles), np.sin(angles)
    cosine, sine = np.concatenate([cosine, cosine], 1), np.concatenate([-sine, sine], 1)
    return jnp.asarray(cosine, jnp.float32), jnp.asarray(sine, jnp.float32)


ANY = pl.BlockSpec(memory_space=pl.ANY)


def combine_kernel(shares, near, far, *rest):
    out = rest[-1]
    mixed = shares[0] * near[...].astype(jnp.float32) + shares[1] * far[...].astype(jnp.float32)
    out[...] = mixed.astype(out.dtype)


def combine(shares, near, far, near_block, width, after=(), cost=0):
    rows, columns = far.shape
    step = min(rows, 512)
    block = pl.BlockSpec((step, width), lambda i, j: (i, j))
    return pl.pallas_call(
        combine_kernel,
        out_shape=jax.ShapeDtypeStruct(far.shape, far.dtype),
        grid=(rows // step, columns // width),
        in_specs=[SMEM, pl.BlockSpec((step, width), lambda i, j: (i, near_block(j))), block]
        + [ANY] * len(after),
        out_specs=block,
        compiler_params=params(),
        cost_estimate=estimate(cost),
    )(shares, near, far, *after)


def columns_kernel(whole, *rest):
    rest[-1][...] = whole[...]


def columns_of(whole, block, width, pieces, after=(), cost=0):
    rows = whole.shape[0]
    step = min(rows, 512)
    return pl.pallas_call(
        columns_kernel,
        out_shape=jax.ShapeDtypeStruct((rows, pieces * width), whole.dtype),
        grid=(rows // step, pieces),
        in_specs=[pl.BlockSpec((step, width), lambda i, j: (i, block(j)))] + [ANY] * len(after),
        out_specs=pl.BlockSpec((step, width), lambda i, j: (i, j)),
        compiler_params=params(),
        cost_estimate=estimate(cost),
    )(whole, *after)


def copy_kernel(source, *rest):
    rest[-1][...] = source[...]


def copied(array, after, cost=0):
    return pl.pallas_call(
        copy_kernel,
        out_shape=jax.ShapeDtypeStruct(array.shape, array.dtype),
        in_specs=[VMEM] + [ANY] * len(after),
        out_specs=VMEM,
        compiler_params=params(),
        cost_estimate=estimate(cost),
    )(array, *after)


def project(ids, blocks, own, other, whole):
    half = own.shape[0]
    mine, place, count = ids[0], ids[1], len(blocks)
    whole[pl.ds(pl.multiple_of(mine * half, half), half), :] = own[...]
    whole[pl.ds(pl.multiple_of((1 - mine) * half, half), half), :] = other[...]
    total = None
    for k, block in enumerate(blocks):
        width = block.shape[1]
        owner = lax.rem(place - k + count, count)
        rows = pl.ds(pl.multiple_of(owner * width, width), width)
        term = jnp.dot(block[...], whole[rows, :], preferred_element_type=jnp.float32)
        total = term if total is None else total + term
    return total


def norm_rope(vectors, cosine, signed_sine):
    meansq = jnp.mean(vectors * vectors, axis=-1, keepdims=True)
    normed = vectors * lax.rsqrt(meansq + EPSILON)
    return normed * cosine + pltpu.roll(normed, HEAD_DIM // 2, 1) * signed_sine


def keyval_kernel(count, ids, *refs):
    blocks = refs[:count]
    own, other, cosine, sine = refs[count : count + 4]
    keys, values, scales, whole = refs[-4:]
    total = 0.0
    features = 0
    for block in blocks:
        rows = block[...].astype(jnp.float32)
        total = total + jnp.sum(rows * rows, axis=-1, keepdims=True)
        features += block.shape[1]
    scale = lax.rsqrt(total / features + EPSILON)
    raw = project(ids, blocks, own, other, whole) * scale
    keys[...] = norm_rope(raw[:, :HEAD_DIM], cosine[...], sine[...]).astype(keys.dtype)
    values[...] = raw[:, HEAD_DIM:].astype(values.dtype)
    scales[...] = jnp.broadcast_to(scale, scales.shape)


def keyval(ids, blocks, own, other, cosine, sine, after=(), cost=0):
    length = blocks[0].shape[0]
    features = sum(b.shape[1] for b in blocks)
    head = jax.ShapeDtypeStruct((length, HEAD_DIM), jnp.bfloat16)
    return pl.pallas_call(
        functools.partial(keyval_kernel, len(blocks)),
        out_shape=(head, head, jax.ShapeDtypeStruct((length, LANES), jnp.float32)),
        in_specs=[SMEM] + [VMEM] * (len(blocks) + 4) + [ANY] * len(after),
        out_specs=(VMEM,) * 3,
        scratch_shapes=[pltpu.VMEM((features, own.shape[1]), own.dtype)],
        compiler_params=params(),
        cost_estimate=estimate(cost),
    )(ids, *blocks, own, other, cosine, sine, *after)


def attend_kernel(count, ids, *refs):
    blocks = refs[:count]
    own, other, keys, values, scales, cosine, sine = refs[count : count + 7]
    mixed, whole = refs[-2:]
    raw = project(ids, blocks, own, other, whole)
    length = raw.shape[0]
    rows = length // 2 if length % 16 == 0 else length
    scale = scales[:, :1]
    for head in range(raw.shape[1] // HEAD_DIM):
        columns = slice(head * HEAD_DIM, (head + 1) * HEAD_DIM)
        query = norm_rope(raw[:, columns] * scale, cosine[...], sine[...]).astype(jnp.bfloat16)
        for first in range(0, length, rows):
            last = first + rows
            scores = lax.dot_general(
                query[first:last],
                keys[:last, :],
                (((1,), (1,)), ((), ())),
                preferred_element_type=jnp.float32,
            )
            expo = jnp.exp(scores * (1.0 / math.sqrt(HEAD_DIM)) - math.sqrt(HEAD_DIM))
            at = first + lax.broadcasted_iota(jnp.int32, expo.shape, 0)
            expo = jnp.where(lax.broadcasted_iota(jnp.int32, expo.shape, 1) <= at, expo, 0.0)
            total = jnp.sum(expo, axis=-1, keepdims=True)
            product = jnp.dot(
                expo.astype(jnp.bfloat16), values[:last, :], preferred_element_type=jnp.float32
            )
            mixed[first:last, columns] = (product / total).astype(mixed.dtype)


def attend(ids, blocks, own, other, keys, values, scales, cosine, sine, after=(), cost=0):
    length = blocks[0].shape[0]
    features = sum(b.shape[1] for b in blocks)
    width = own.shape[1]
    return pl.pallas_call(
        functools.partial(attend_kernel, len(blocks)),
        out_shape=jax.ShapeDtypeStruct((length, width), jnp.bfloat16),
        in_specs=[SMEM] + [VMEM] * (len(blocks) + 7) + [ANY] * len(after),
        out_specs=VMEM,
        scratch_shapes=[pltpu.VMEM((features, width), own.dtype)],
        compiler_params=params(),
        cost_estimate=estimate(cost),
    )(ids, *blocks, own, other, keys, values, scales, cosine, sine, *after)


def products(ids, mixed, own, other, by_owner):
    mine = ids[0]
    count, _, width = by_owner.shape
    per_half = count // 2
    for half, weights in ((mine, own), (1 - mine, other)):
        total = None
        depth = 0
        for part in mixed:
            rows = slice(depth, depth + part.shape[1])
            depth += part.shape[1]
            term = jnp.dot(part[...], weights[rows, :], preferred_element_type=jnp.float32)
            total = term if total is None else total + term
        for piece in range(per_half):
            by_owner[half * per_half + piece] = total[
                :, piece * width : (piece + 1) * width
            ].astype(by_owner.dtype)


def partial_kernel(count, parts, ids, *refs):
    kept, sent, by_owner = refs[-3:]
    products(ids, refs[:parts], refs[parts], refs[parts + 1], by_owner)
    low = lax.rem(ids[1], 2)
    for pair in range(count // 2):
        kept[pair] = by_owner[2 * pair + low]
        sent[pair] = by_owner[2 * pair + 1 - low]


def direct_kernel(count, parts, ids, *refs):
    outs, by_owner = refs[-1 - count : -1], refs[-1]
    products(ids, refs[:parts], refs[parts], refs[parts + 1], by_owner)
    for k in range(count):
        outs[k][...] = by_owner[lax.rem(ids[1] + k, count)]


def direct_partials(ids, mixed, own, other, count, after=(), cost=0):
    length = mixed[0].shape[0]
    width = 2 * own.shape[1] // count
    piece = jax.ShapeDtypeStruct((length, width), jnp.bfloat16)
    return pl.pallas_call(
        functools.partial(direct_kernel, count, len(mixed)),
        out_shape=(piece,) * count,
        in_specs=[SMEM] + [VMEM] * (len(mixed) + 2) + [ANY] * len(after),
        out_specs=(VMEM,) * count,
        scratch_shapes=[pltpu.VMEM((count, length, width), jnp.bfloat16)],
        compiler_params=params(),
        cost_estimate=estimate(cost),
    )(ids, *mixed, own, other, *after)


def partials(ids, mixed, own, other, count, after=(), cost=0):
    length = mixed[0].shape[0]
    width = 2 * own.shape[1] // count
    half = jax.ShapeDtypeStruct((count // 2, length, width), jnp.bfloat16)
    return pl.pallas_call(
        functools.partial(partial_kernel, count, len(mixed)),
        out_shape=(half, half),
        in_specs=[SMEM] + [VMEM] * (len(mixed) + 2) + [ANY] * len(after),
        out_specs=(VMEM, VMEM),
        scratch_shapes=[pltpu.VMEM((count, length, width), jnp.bfloat16)],
        compiler_params=params(),
        cost_estimate=estimate(cost),
    )(ids, *mixed, own, other, *after)


def reduce_kernel(ids, kept, got, *refs):
    still, sent = refs[-2:]
    high = lax.rem(lax.div(ids[1], 2), 2)
    still[...] = kept[high].astype(jnp.float32) + got[high].astype(jnp.float32)
    away = kept[1 - high].astype(jnp.float32) + got[1 - high].astype(jnp.float32)
    sent[...] = away.astype(sent.dtype)


def reduce(ids, kept, got, after=(), cost=0):
    shape = kept.shape[1:]
    return pl.pallas_call(
        reduce_kernel,
        out_shape=(
            jax.ShapeDtypeStruct(shape, jnp.float32),
            jax.ShapeDtypeStruct(shape, jnp.bfloat16),
        ),
        in_specs=[SMEM, VMEM, VMEM] + [ANY] * len(after),
        out_specs=(VMEM, VMEM),
        compiler_params=params(),
        cost_estimate=estimate(cost),
    )(ids, kept, got, *after)


def leave_kernel(counts, rows, *refs):
    out = refs[-1]
    width = rows.shape[1] // len(counts)
    first = 0
    for chunk, count in enumerate(counts):
        columns = slice(chunk * width, (chunk + 1) * width)
        total = rows[:, columns].astype(jnp.float32)
        for piece in refs[first : first + count]:
            total = total + piece[...].astype(jnp.float32)
        first += count
        out[:, columns] = total.astype(out.dtype)


def leave(rows, pieces):
    flat = [piece for chunk in pieces for piece in chunk]
    return pl.pallas_call(
        functools.partial(leave_kernel, [len(chunk) for chunk in pieces]),
        out_shape=jax.ShapeDtypeStruct(rows.shape, rows.dtype),
        in_specs=[VMEM] * (1 + len(flat)),
        out_specs=VMEM,
        compiler_params=params(),
        cost_estimate=estimate(1),
    )(rows, *flat)


def permute(array, axis, source):
    count = lax.axis_size(axis)
    return lax.ppermute(array, axis, [(source(i) % count, i) for i in range(count)])


def from_near(array):
    return permute(array, "section", lambda i: i ^ 1)


def from_far(array):
    return permute(array, "section", lambda i: i + 1 if i % 2 else i - 1)


def from_other_half(array):
    return permute(array, "fsdp", lambda i: i ^ 1)


def body(entering, w_query, w_keyval, w_out):
    count = lax.axis_size("tensor")
    section = lax.axis_index("section")
    ids = jnp.stack([lax.axis_index("fsdp"), lax.axis_index("tensor")]).astype(jnp.int32)
    shares = jnp.where(
        section % 2 == 0,
        jnp.array([AFTER_SHARE, BEFORE_SHARE], jnp.float32),
        jnp.array([BEFORE_SHARE, AFTER_SHARE], jnp.float32),
    )
    rows = entering[0]
    length = rows.shape[0]
    own_query = w_query[0]
    own_keyval = w_keyval.reshape(w_keyval.shape[1], -1)
    own_out = w_out[0]
    query_width = own_query.shape[1] // QUERY_CHUNKS
    halves = count // 2
    quarter = own_out.shape[1] // halves
    out_width = quarter // OUT_CHUNKS

    near_keyval, near_query, near_out = map(from_near, (own_keyval, own_query, own_out))
    far = {0: from_far(own_keyval)}
    places = [(own_keyval, near_keyval, own_keyval.shape[1], lambda j: 0)]
    for c in range(QUERY_CHUNKS):
        places.append((own_query, near_query, query_width, lambda j, c=c: c))
    for c in range(OUT_CHUNKS):
        places.append((own_out, near_out, out_width, lambda j, c=c: j * OUT_CHUNKS + c))
    pieces_of = [1] * (1 + QUERY_CHUNKS) + [halves] * OUT_CHUNKS
    blocks = [rows] + [None] * (count - 1)
    for k in FIRST:
        blocks[k] = permute(rows, "tensor", lambda i, k=k: i - k)
    cosine, sine = rope_tables(length, HEAD_DIM)

    own, other, mixed, halves_of, pieces, before = {}, {}, [], {}, {}, []
    for kind, c, arrivals, cost in STEPS:
        after = list(before)
        for name in arrivals.split():
            if name[0] == "y":
                after.append(other[int(name[1:])])
            elif name[0] == "a":
                after.append(blocks[int(name[1:])])
            elif name[0] == "n":
                after.append((near_query, near_out)[int(name[1:])])
            elif name[0] == "s":
                after.append(halves_of[int(name[1:])][1])
            else:
                after.append(pieces[int(name[1:])][1])
        if kind == "G":
            whole, _, width, place = places[c]
            chunk = columns_of(whole, place, width, pieces_of[c], after=after, cost=cost)
            far[c] = from_far(chunk)
            before = [chunk]
        elif kind == "C":
            _, near, width, place = places[c]
            own[c] = combine(shares, near, far[c], place, width, after=after, cost=cost)
            other[c] = from_other_half(own[c])
            before = [own[c]]
        elif kind == "X":
            again = copied(rows, after=after + [blocks[k] for k in FIRST], cost=cost)
            for k in range(1, count):
                if k not in FIRST:
                    blocks[k] = permute(again, "tensor", lambda i, k=k: i - k)
            before = [again]
        elif kind == "K":
            keys, values, scales = keyval(
                ids, blocks, own[c], other[c], cosine, sine, after=after, cost=cost
            )
            before = [scales]
        elif kind == "A":
            mixed.append(
                attend(
                    ids,
                    blocks,
                    own[c],
                    other[c],
                    keys,
                    values,
                    scales,
                    cosine,
                    sine,
                    after=after,
                    cost=cost,
                )
            )
            before = [mixed[-1]]
        elif kind == "P":
            kept, sent = partials(
                ids, mixed, own[c], other[c], count, after=after, cost=cost
            )
            halves_of[c] = (kept, permute(sent, "tensor", lambda i: i ^ 1))
            before = [kept]
        elif kind == "Q":
            parts = direct_partials(
                ids, mixed, own[c], other[c], count, after=after, cost=cost
            )
            pieces[c] = [parts[0]] + [
                permute(parts[k], "tensor", lambda i, k=k: i - k) for k in range(1, count)
            ]
            before = [parts[0]]
        else:
            kept, sent = reduce(ids, *halves_of[c], after=after, cost=cost)
            pieces[c] = (kept, permute(sent, "tensor", lambda i: i ^ 2))
            before = [kept]
    pieces = [pieces[c] for c in sorted(pieces)]
    return leave(rows, pieces)[None]


def shifted(block, axis, distance):
    return permute(block, axis, lambda i: i - distance)


def head_norm_rope(vectors, cosine, signed_sine):
    meansq = jnp.mean(vectors * vectors, axis=-1, keepdims=True)
    normed = vectors * lax.rsqrt(meansq + EPSILON)
    return normed * cosine + jnp.roll(normed, vectors.shape[-1] // 2, axis=-1) * signed_sine


def rebuilt(weights):
    before = shifted(weights, "section", 1).astype(jnp.float32)
    after = shifted(weights, "section", -1).astype(jnp.float32)
    return (BEFORE_SHARE * before + AFTER_SHARE * after).astype(jnp.bfloat16)


def general_body(entering, w_query, w_keyval, w_out):
    rows = entering[0].astype(jnp.float32)
    features = rows.shape[1] * lax.axis_size("tensor")
    square_total = lax.psum(jnp.sum(rows * rows, axis=-1, keepdims=True), "tensor")
    normed = (rows * lax.rsqrt(square_total / features + EPSILON)).astype(jnp.bfloat16)
    normed = lax.all_gather(normed, "tensor", axis=1, tiled=True)
    length = normed.shape[0]
    query_weight = lax.all_gather(rebuilt(w_query)[0], "fsdp", axis=0, tiled=True)
    keyval_weight = lax.all_gather(rebuilt(w_keyval)[0], "fsdp", axis=0, tiled=True)
    out_weight = lax.all_gather(rebuilt(w_out)[0], "fsdp", axis=1, tiled=True)
    kv_count = keyval_weight.shape[1]
    raw = jnp.dot(normed, query_weight, preferred_element_type=jnp.float32)
    raw = raw.reshape(length, kv_count, -1, HEAD_DIM)
    keyval_raw = jnp.dot(
        normed, keyval_weight.reshape(features, -1), preferred_element_type=jnp.float32
    ).reshape(length, kv_count, 2 * HEAD_DIM)
    cosine, sine = rope_tables(length, HEAD_DIM)
    queries = head_norm_rope(raw, cosine[:, None, None], sine[:, None, None]).astype(jnp.bfloat16)
    keys = head_norm_rope(
        keyval_raw[..., :HEAD_DIM], cosine[:, None], sine[:, None]
    ).astype(jnp.bfloat16)
    values = keyval_raw[..., HEAD_DIM:].astype(jnp.bfloat16)
    causal = jnp.arange(length)[:, None] >= jnp.arange(length)[None, :]

    def one_group(query_slice):
        scores = jnp.einsum("qkd,pkd->kqp", query_slice, keys, preferred_element_type=jnp.float32)
        expo = jnp.exp(scores * (1.0 / math.sqrt(HEAD_DIM)) - math.sqrt(HEAD_DIM))
        expo = jnp.where(causal[None], expo, 0.0)
        weights = (expo / jnp.sum(expo, axis=-1, keepdims=True)).astype(jnp.bfloat16)
        return jnp.einsum(
            "kqp,pkd->qkd", weights, values, preferred_element_type=jnp.float32
        ).astype(jnp.bfloat16)

    mixed = lax.map(one_group, jnp.moveaxis(queries, 2, 0))
    mixed = jnp.moveaxis(mixed, 0, 2).reshape(length, -1)
    terms = jnp.dot(mixed, out_weight, preferred_element_type=jnp.float32).astype(jnp.bfloat16)
    summed = lax.psum_scatter(terms, "tensor", scatter_dimension=1, tiled=True)
    return (rows + summed.astype(jnp.float32)).astype(jnp.bfloat16)[None]


def solution(mesh):
    in_specs = (
        P("section", "fsdp", "tensor"),
        P("section", "fsdp", "tensor"),
        P("section", "fsdp", "tensor", None),
        P("section", "tensor", "fsdp"),
    )
    out_specs = P("section", "fsdp", "tensor")

    def step(entering, w_query, w_keyval, w_out):
        chunked = (
            mesh.shape["section"] % 2 == 0
            and mesh.shape["fsdp"] == 2
            and mesh.shape["tensor"] == 4
            and w_keyval.shape[2] == mesh.shape["tensor"]
            and w_keyval.shape[3] == 2 * HEAD_DIM
            and w_query.shape[2] % (mesh.shape["tensor"] * QUERY_CHUNKS * HEAD_DIM) == 0
            and w_out.shape[2] % (mesh.shape["tensor"] * OUT_CHUNKS * LANES) == 0
        )
        return jax.shard_map(
            body if chunked else general_body,
            mesh=mesh,
            in_specs=in_specs,
            out_specs=out_specs,
            check_vma=False,
        )(entering, w_query, w_keyval, w_out)

    return step
```

```python
import functools
import math

import jax
import jax.numpy as jnp
import numpy as np
from jax import lax
from jax.experimental import pallas as pl
from jax.experimental.pallas import tpu as pltpu
from jax.sharding import PartitionSpec as P

HEAD_DIM = 128
EPSILON = 1e-06
ROPE_BASE = 1000000.0
BEFORE_SHARE = 0.6
AFTER_SHARE = 0.4
LANES = 128
VMEM_BYTES = 48 * 1024 * 1024
QUERY_CHUNKS = 4
OUT_CHUNKS = 4
FIRST = (1, 3)
STEPS = (('G', 2, '', 1500), ('G', 1, 'n1', 700), ('G', 3, '', 3000), ('C', 0, '', 700), ('C', 1, '', 700), ('X', 0, '', 1000), ('G', 4, '', 50), ('C', 2, 'y0', 700), ('C', 3, 'y1', 700), ('G', 5, '', 4000), ('G', 6, '', 50), ('K', 0, '', 4000), ('C', 4, '', 700), ('A', 1, 'n0', 4000), ('A', 2, '', 700), ('G', 7, '', 1000), ('C', 5, 'y2', 700), ('A', 3, '', 4000), ('C', 6, 'a3', 700), ('A', 4, '', 1500), ('P', 5, '', 2000), ('G', 8, '', 50), ('C', 7, '', 700), ('R', 5, 'a2 y5 y6', 0), ('P', 6, '', 2000), ('C', 8, '', 700), ('P', 7, 't5 y3', 6000), ('R', 6, 'y4', 700), ('R', 7, 'a1 s7', 1500), ('Q', 8, '', 50))

SMEM = pl.BlockSpec(memory_space=pltpu.SMEM)
VMEM = pl.BlockSpec(memory_space=pltpu.VMEM)


def estimate(cost):
    return pl.CostEstimate(flops=cost * 2**20, bytes_accessed=0, transcendentals=0)


def params():
    return pltpu.CompilerParams(vmem_limit_bytes=VMEM_BYTES)


def rope_tables(length, width):
    inverse = ROPE_BASE ** (np.arange(width // 2) * (-2.0 / width))
    angles = np.arange(length)[:, None] * inverse[None, :]
    cosine, sine = np.cos(angles), np.sin(angles)
    cosine, sine = np.concatenate([cosine, cosine], 1), np.concatenate([-sine, sine], 1)
    return jnp.asarray(cosine, jnp.float32), jnp.asarray(sine, jnp.float32)


ANY = pl.BlockSpec(memory_space=pl.ANY)


def combine_kernel(shares, near, far, *rest):
    out = rest[-1]
    mixed = shares[0] * near[...].astype(jnp.float32) + shares[1] * far[...].astype(jnp.float32)
    out[...] = mixed.astype(out.dtype)


def combine(shares, near, far, near_block, width, after=(), cost=0):
    rows, columns = far.shape
    step = min(rows, 512)
    block = pl.BlockSpec((step, width), lambda i, j: (i, j))
    return pl.pallas_call(
        combine_kernel,
        out_shape=jax.ShapeDtypeStruct(far.shape, far.dtype),
        grid=(rows // step, columns // width),
        in_specs=[SMEM, pl.BlockSpec((step, width), lambda i, j: (i, near_block(j))), block]
        + [ANY] * len(after),
        out_specs=block,
        compiler_params=params(),
        cost_estimate=estimate(cost),
    )(shares, near, far, *after)


def columns_kernel(whole, *rest):
    rest[-1][...] = whole[...]


def columns_of(whole, block, width, pieces, after=(), cost=0):
    rows = whole.shape[0]
    step = min(rows, 512)
    return pl.pallas_call(
        columns_kernel,
        out_shape=jax.ShapeDtypeStruct((rows, pieces * width), whole.dtype),
        grid=(rows // step, pieces),
        in_specs=[pl.BlockSpec((step, width), lambda i, j: (i, block(j)))] + [ANY] * len(after),
        out_specs=pl.BlockSpec((step, width), lambda i, j: (i, j)),
        compiler_params=params(),
        cost_estimate=estimate(cost),
    )(whole, *after)


def copy_kernel(source, *rest):
    rest[-1][...] = source[...]


def copied(array, after, cost=0):
    return pl.pallas_call(
        copy_kernel,
        out_shape=jax.ShapeDtypeStruct(array.shape, array.dtype),
        in_specs=[VMEM] + [ANY] * len(after),
        out_specs=VMEM,
        compiler_params=params(),
        cost_estimate=estimate(cost),
    )(array, *after)


def project(ids, blocks, own, other, whole):
    half = own.shape[0]
    mine, place, count = ids[0], ids[1], len(blocks)
    whole[pl.ds(pl.multiple_of(mine * half, half), half), :] = own[...]
    whole[pl.ds(pl.multiple_of((1 - mine) * half, half), half), :] = other[...]
    total = None
    for k, block in enumerate(blocks):
        width = block.shape[1]
        owner = lax.rem(place - k + count, count)
        rows = pl.ds(pl.multiple_of(owner * width, width), width)
        term = jnp.dot(block[...], whole[rows, :], preferred_element_type=jnp.float32)
        total = term if total is None else total + term
    return total


def norm_rope(vectors, cosine, signed_sine):
    meansq = jnp.mean(vectors * vectors, axis=-1, keepdims=True)
    normed = vectors * lax.rsqrt(meansq + EPSILON)
    return normed * cosine + pltpu.roll(normed, HEAD_DIM // 2, 1) * signed_sine


def keyval_kernel(count, ids, *refs):
    blocks = refs[:count]
    own, other, cosine, sine = refs[count : count + 4]
    keys, values, scales, whole = refs[-4:]
    total = 0.0
    features = 0
    for block in blocks:
        rows = block[...].astype(jnp.float32)
        total = total + jnp.sum(rows * rows, axis=-1, keepdims=True)
        features += block.shape[1]
    scale = lax.rsqrt(total / features + EPSILON)
    raw = project(ids, blocks, own, other, whole) * scale
    keys[...] = norm_rope(raw[:, :HEAD_DIM], cosine[...], sine[...]).astype(keys.dtype)
    values[...] = raw[:, HEAD_DIM:].astype(values.dtype)
    scales[...] = jnp.broadcast_to(scale, scales.shape)


def keyval(ids, blocks, own, other, cosine, sine, after=(), cost=0):
    length = blocks[0].shape[0]
    features = sum(b.shape[1] for b in blocks)
    head = jax.ShapeDtypeStruct((length, HEAD_DIM), jnp.bfloat16)
    return pl.pallas_call(
        functools.partial(keyval_kernel, len(blocks)),
        out_shape=(head, head, jax.ShapeDtypeStruct((length, LANES), jnp.float32)),
        in_specs=[SMEM] + [VMEM] * (len(blocks) + 4) + [ANY] * len(after),
        out_specs=(VMEM,) * 3,
        scratch_shapes=[pltpu.VMEM((features, own.shape[1]), own.dtype)],
        compiler_params=params(),
        cost_estimate=estimate(cost),
    )(ids, *blocks, own, other, cosine, sine, *after)


def attend_kernel(count, ids, *refs):
    blocks = refs[:count]
    own, other, keys, values, scales, cosine, sine = refs[count : count + 7]
    mixed, whole = refs[-2:]
    raw = project(ids, blocks, own, other, whole)
    length = raw.shape[0]
    rows = length // 2 if length % 16 == 0 else length
    scale = scales[:, :1]
    for head in range(raw.shape[1] // HEAD_DIM):
        columns = slice(head * HEAD_DIM, (head + 1) * HEAD_DIM)
        query = norm_rope(raw[:, columns] * scale, cosine[...], sine[...]).astype(jnp.bfloat16)
        for first in range(0, length, rows):
            last = first + rows
            scores = lax.dot_general(
                query[first:last],
                keys[:last, :],
                (((1,), (1,)), ((), ())),
                preferred_element_type=jnp.float32,
            )
            expo = jnp.exp(scores * (1.0 / math.sqrt(HEAD_DIM)) - math.sqrt(HEAD_DIM))
            at = first + lax.broadcasted_iota(jnp.int32, expo.shape, 0)
            expo = jnp.where(lax.broadcasted_iota(jnp.int32, expo.shape, 1) <= at, expo, 0.0)
            total = jnp.sum(expo, axis=-1, keepdims=True)
            product = jnp.dot(
                expo.astype(jnp.bfloat16), values[:last, :], preferred_element_type=jnp.float32
            )
            mixed[first:last, columns] = (product / total).astype(mixed.dtype)


def attend(ids, blocks, own, other, keys, values, scales, cosine, sine, after=(), cost=0):
    length = blocks[0].shape[0]
    features = sum(b.shape[1] for b in blocks)
    width = own.shape[1]
    return pl.pallas_call(
        functools.partial(attend_kernel, len(blocks)),
        out_shape=jax.ShapeDtypeStruct((length, width), jnp.bfloat16),
        in_specs=[SMEM] + [VMEM] * (len(blocks) + 7) + [ANY] * len(after),
        out_specs=VMEM,
        scratch_shapes=[pltpu.VMEM((features, width), own.dtype)],
        compiler_params=params(),
        cost_estimate=estimate(cost),
    )(ids, *blocks, own, other, keys, values, scales, cosine, sine, *after)


def products(ids, mixed, own, other, by_owner):
    mine = ids[0]
    count, _, width = by_owner.shape
    per_half = count // 2
    for half, weights in ((mine, own), (1 - mine, other)):
        total = None
        depth = 0
        for part in mixed:
            rows = slice(depth, depth + part.shape[1])
            depth += part.shape[1]
            term = jnp.dot(part[...], weights[rows, :], preferred_element_type=jnp.float32)
            total = term if total is None else total + term
        for piece in range(per_half):
            by_owner[half * per_half + piece] = total[
                :, piece * width : (piece + 1) * width
            ].astype(by_owner.dtype)


def partial_kernel(count, parts, ids, *refs):
    kept, sent, by_owner = refs[-3:]
    products(ids, refs[:parts], refs[parts], refs[parts + 1], by_owner)
    low = lax.rem(ids[1], 2)
    for pair in range(count // 2):
        kept[pair] = by_owner[2 * pair + low]
        sent[pair] = by_owner[2 * pair + 1 - low]


def direct_kernel(count, parts, ids, *refs):
    outs, by_owner = refs[-1 - count : -1], refs[-1]
    products(ids, refs[:parts], refs[parts], refs[parts + 1], by_owner)
    for k in range(count):
        outs[k][...] = by_owner[lax.rem(ids[1] + k, count)]


def direct_partials(ids, mixed, own, other, count, after=(), cost=0):
    length = mixed[0].shape[0]
    width = 2 * own.shape[1] // count
    piece = jax.ShapeDtypeStruct((length, width), jnp.bfloat16)
    return pl.pallas_call(
        functools.partial(direct_kernel, count, len(mixed)),
        out_shape=(piece,) * count,
        in_specs=[SMEM] + [VMEM] * (len(mixed) + 2) + [ANY] * len(after),
        out_specs=(VMEM,) * count,
        scratch_shapes=[pltpu.VMEM((count, length, width), jnp.bfloat16)],
        compiler_params=params(),
        cost_estimate=estimate(cost),
    )(ids, *mixed, own, other, *after)


def partials(ids, mixed, own, other, count, after=(), cost=0):
    length = mixed[0].shape[0]
    width = 2 * own.shape[1] // count
    half = jax.ShapeDtypeStruct((count // 2, length, width), jnp.bfloat16)
    return pl.pallas_call(
        functools.partial(partial_kernel, count, len(mixed)),
        out_shape=(half, half),
        in_specs=[SMEM] + [VMEM] * (len(mixed) + 2) + [ANY] * len(after),
        out_specs=(VMEM, VMEM),
        scratch_shapes=[pltpu.VMEM((count, length, width), jnp.bfloat16)],
        compiler_params=params(),
        cost_estimate=estimate(cost),
    )(ids, *mixed, own, other, *after)


def reduce_kernel(ids, kept, got, *refs):
    still, sent = refs[-2:]
    high = lax.rem(lax.div(ids[1], 2), 2)
    still[...] = kept[high].astype(jnp.float32) + got[high].astype(jnp.float32)
    away = kept[1 - high].astype(jnp.float32) + got[1 - high].astype(jnp.float32)
    sent[...] = away.astype(sent.dtype)


def reduce(ids, kept, got, after=(), cost=0):
    shape = kept.shape[1:]
    return pl.pallas_call(
        reduce_kernel,
        out_shape=(
            jax.ShapeDtypeStruct(shape, jnp.float32),
            jax.ShapeDtypeStruct(shape, jnp.bfloat16),
        ),
        in_specs=[SMEM, VMEM, VMEM] + [ANY] * len(after),
        out_specs=(VMEM, VMEM),
        compiler_params=params(),
        cost_estimate=estimate(cost),
    )(ids, kept, got, *after)


def leave_kernel(counts, rows, *refs):
    out = refs[-1]
    width = rows.shape[1] // len(counts)
    first = 0
    for chunk, count in enumerate(counts):
        columns = slice(chunk * width, (chunk + 1) * width)
        total = rows[:, columns].astype(jnp.float32)
        for piece in refs[first : first + count]:
            total = total + piece[...].astype(jnp.float32)
        first += count
        out[:, columns] = total.astype(out.dtype)


def leave(rows, pieces):
    flat = [piece for chunk in pieces for piece in chunk]
    return pl.pallas_call(
        functools.partial(leave_kernel, [len(chunk) for chunk in pieces]),
        out_shape=jax.ShapeDtypeStruct(rows.shape, rows.dtype),
        in_specs=[VMEM] * (1 + len(flat)),
        out_specs=VMEM,
        compiler_params=params(),
        cost_estimate=estimate(1),
    )(rows, *flat)


def permute(array, axis, source):
    count = lax.axis_size(axis)
    return lax.ppermute(array, axis, [(source(i) % count, i) for i in range(count)])


def from_near(array):
    return permute(array, "section", lambda i: i ^ 1)


def from_far(array):
    return permute(array, "section", lambda i: i + 1 if i % 2 else i - 1)


def from_other_half(array):
    return permute(array, "fsdp", lambda i: i ^ 1)


def body(entering, w_query, w_keyval, w_out):
    count = lax.axis_size("tensor")
    section = lax.axis_index("section")
    ids = jnp.stack([lax.axis_index("fsdp"), lax.axis_index("tensor")]).astype(jnp.int32)
    shares = jnp.where(
        section % 2 == 0,
        jnp.array([AFTER_SHARE, BEFORE_SHARE], jnp.float32),
        jnp.array([BEFORE_SHARE, AFTER_SHARE], jnp.float32),
    )
    rows = entering[0]
    length = rows.shape[0]
    own_query = w_query[0]
    own_keyval = w_keyval.reshape(w_keyval.shape[1], -1)
    own_out = w_out[0]
    query_width = own_query.shape[1] // QUERY_CHUNKS
    halves = count // 2
    quarter = own_out.shape[1] // halves
    out_width = quarter // OUT_CHUNKS

    near_keyval, near_query, near_out = map(from_near, (own_keyval, own_query, own_out))
    far = {0: from_far(own_keyval)}
    places = [(own_keyval, near_keyval, own_keyval.shape[1], lambda j: 0)]
    for c in range(QUERY_CHUNKS):
        places.append((own_query, near_query, query_width, lambda j, c=c: c))
    for c in range(OUT_CHUNKS):
        places.append((own_out, near_out, out_width, lambda j, c=c: j * OUT_CHUNKS + c))
    pieces_of = [1] * (1 + QUERY_CHUNKS) + [halves] * OUT_CHUNKS
    blocks = [rows] + [None] * (count - 1)
    for k in FIRST:
        blocks[k] = permute(rows, "tensor", lambda i, k=k: i - k)
    cosine, sine = rope_tables(length, HEAD_DIM)

    own, other, mixed, halves_of, pieces, before = {}, {}, [], {}, {}, []
    for kind, c, arrivals, cost in STEPS:
        after = list(before)
        for name in arrivals.split():
            if name[0] == "y":
                after.append(other[int(name[1:])])
            elif name[0] == "a":
                after.append(blocks[int(name[1:])])
            elif name[0] == "n":
                after.append((near_query, near_out)[int(name[1:])])
            elif name[0] == "s":
                after.append(halves_of[int(name[1:])][1])
            else:
                after.append(pieces[int(name[1:])][1])
        if kind == "G":
            whole, _, width, place = places[c]
            chunk = columns_of(whole, place, width, pieces_of[c], after=after, cost=cost)
            far[c] = from_far(chunk)
            before = [chunk]
        elif kind == "C":
            _, near, width, place = places[c]
            own[c] = combine(shares, near, far[c], place, width, after=after, cost=cost)
            other[c] = from_other_half(own[c])
            before = [own[c]]
        elif kind == "X":
            again = copied(rows, after=after + [blocks[k] for k in FIRST], cost=cost)
            for k in range(1, count):
                if k not in FIRST:
                    blocks[k] = permute(again, "tensor", lambda i, k=k: i - k)
            before = [again]
        elif kind == "K":
            keys, values, scales = keyval(
                ids, blocks, own[c], other[c], cosine, sine, after=after, cost=cost
            )
            before = [scales]
        elif kind == "A":
            mixed.append(
                attend(
                    ids,
                    blocks,
                    own[c],
                    other[c],
                    keys,
                    values,
                    scales,
                    cosine,
                    sine,
                    after=after,
                    cost=cost,
                )
            )
            before = [mixed[-1]]
        elif kind == "P":
            kept, sent = partials(
                ids, mixed, own[c], other[c], count, after=after, cost=cost
            )
            halves_of[c] = (kept, permute(sent, "tensor", lambda i: i ^ 1))
            before = [kept]
        elif kind == "Q":
            parts = direct_partials(
                ids, mixed, own[c], other[c], count, after=after, cost=cost
            )
            pieces[c] = [parts[0]] + [
                permute(parts[k], "tensor", lambda i, k=k: i - k) for k in range(1, count)
            ]
            before = [parts[0]]
        else:
            kept, sent = reduce(ids, *halves_of[c], after=after, cost=cost)
            pieces[c] = (kept, permute(sent, "tensor", lambda i: i ^ 2))
            before = [kept]
    pieces = [pieces[c] for c in sorted(pieces)]
    return leave(rows, pieces)[None]


def shifted(block, axis, distance):
    return permute(block, axis, lambda i: i - distance)


def head_norm_rope(vectors, cosine, signed_sine):
    meansq = jnp.mean(vectors * vectors, axis=-1, keepdims=True)
    normed = vectors * lax.rsqrt(meansq + EPSILON)
    return normed * cosine + jnp.roll(normed, vectors.shape[-1] // 2, axis=-1) * signed_sine


def rebuilt(weights):
    before = shifted(weights, "section", 1).astype(jnp.float32)
    after = shifted(weights, "section", -1).astype(jnp.float32)
    return (BEFORE_SHARE * before + AFTER_SHARE * after).astype(jnp.bfloat16)


def general_body(entering, w_query, w_keyval, w_out):
    rows = entering[0].astype(jnp.float32)
    features = rows.shape[1] * lax.axis_size("tensor")
    square_total = lax.psum(jnp.sum(rows * rows, axis=-1, keepdims=True), "tensor")
    normed = (rows * lax.rsqrt(square_total / features + EPSILON)).astype(jnp.bfloat16)
    normed = lax.all_gather(normed, "tensor", axis=1, tiled=True)
    length = normed.shape[0]
    query_weight = lax.all_gather(rebuilt(w_query)[0], "fsdp", axis=0, tiled=True)
    keyval_weight = lax.all_gather(rebuilt(w_keyval)[0], "fsdp", axis=0, tiled=True)
    out_weight = lax.all_gather(rebuilt(w_out)[0], "fsdp", axis=1, tiled=True)
    kv_count = keyval_weight.shape[1]
    raw = jnp.dot(normed, query_weight, preferred_element_type=jnp.float32)
    raw = raw.reshape(length, kv_count, -1, HEAD_DIM)
    keyval_raw = jnp.dot(
        normed, keyval_weight.reshape(features, -1), preferred_element_type=jnp.float32
    ).reshape(length, kv_count, 2 * HEAD_DIM)
    cosine, sine = rope_tables(length, HEAD_DIM)
    queries = head_norm_rope(raw, cosine[:, None, None], sine[:, None, None]).astype(jnp.bfloat16)
    keys = head_norm_rope(
        keyval_raw[..., :HEAD_DIM], cosine[:, None], sine[:, None]
    ).astype(jnp.bfloat16)
    values = keyval_raw[..., HEAD_DIM:].astype(jnp.bfloat16)
    causal = jnp.arange(length)[:, None] >= jnp.arange(length)[None, :]

    def one_group(query_slice):
        scores = jnp.einsum("qkd,pkd->kqp", query_slice, keys, preferred_element_type=jnp.float32)
        expo = jnp.exp(scores * (1.0 / math.sqrt(HEAD_DIM)) - math.sqrt(HEAD_DIM))
        expo = jnp.where(causal[None], expo, 0.0)
        weights = (expo / jnp.sum(expo, axis=-1, keepdims=True)).astype(jnp.bfloat16)
        return jnp.einsum(
            "kqp,pkd->qkd", weights, values, preferred_element_type=jnp.float32
        ).astype(jnp.bfloat16)

    mixed = lax.map(one_group, jnp.moveaxis(queries, 2, 0))
    mixed = jnp.moveaxis(mixed, 0, 2).reshape(length, -1)
    terms = jnp.dot(mixed, out_weight, preferred_element_type=jnp.float32).astype(jnp.bfloat16)
    summed = lax.psum_scatter(terms, "tensor", scatter_dimension=1, tiled=True)
    return (rows + summed.astype(jnp.float32)).astype(jnp.bfloat16)[None]


def solution(mesh):
    in_specs = (
        P("section", "fsdp", "tensor"),
        P("section", "fsdp", "tensor"),
        P("section", "fsdp", "tensor", None),
        P("section", "tensor", "fsdp"),
    )
    out_specs = P("section", "fsdp", "tensor")

    def step(entering, w_query, w_keyval, w_out):
        chunked = (
            mesh.shape["section"] % 2 == 0
            and mesh.shape["fsdp"] == 2
            and mesh.shape["tensor"] == 4
            and w_keyval.shape[2] == mesh.shape["tensor"]
            and w_keyval.shape[3] == 2 * HEAD_DIM
            and w_query.shape[2] % (mesh.shape["tensor"] * QUERY_CHUNKS * HEAD_DIM) == 0
            and w_out.shape[2] % (mesh.shape["tensor"] * OUT_CHUNKS * LANES) == 0
        )
        return jax.shard_map(
            body if chunked else general_body,
            mesh=mesh,
            in_specs=in_specs,
            out_specs=out_specs,
            check_vma=False,
        )(entering, w_query, w_keyval, w_out)

    return step
```

```python
import functools
import math

import jax
import jax.numpy as jnp
import numpy as np
from jax import lax
from jax.experimental import pallas as pl
from jax.experimental.pallas import tpu as pltpu
from jax.sharding import PartitionSpec as P

HEAD_DIM = 128
EPSILON = 1e-06
ROPE_BASE = 1000000.0
BEFORE_SHARE = 0.6
AFTER_SHARE = 0.4
LANES = 128
VMEM_BYTES = 48 * 1024 * 1024
QUERY_CHUNKS = 4
OUT_CHUNKS = 4
FIRST = (1, 3)
STEPS = (('G', 1, 'n1', 6000), ('G', 2, '', 6000), ('C', 0, '', 700), ('G', 3, '', 6000), ('C', 1, '', 4000), ('X', 0, '', 200), ('G', 4, '', 6000), ('C', 2, '', 0), ('G', 5, 'y0', 6000), ('C', 3, 'y1', 4000), ('K', 0, '', 6000), ('G', 6, '', 6000), ('C', 4, '', 0), ('A', 1, 'a1', 0), ('A', 2, 'a3', 2000), ('A', 3, '', 1000), ('C', 5, '', 4000), ('A', 4, '', 2000), ('G', 8, '', 6000), ('G', 7, '', 6000), ('C', 6, '', 0), ('P', 5, '', 3000), ('C', 7, '', 4000), ('R', 5, 'y3', 1000), ('P', 6, '', 6000), ('C', 8, '', 0), ('P', 7, 't5', 3000), ('R', 6, 'y4', 50), ('R', 7, '', 1000), ('Q', 8, 'a2', 4000))

SMEM = pl.BlockSpec(memory_space=pltpu.SMEM)
VMEM = pl.BlockSpec(memory_space=pltpu.VMEM)


def estimate(cost):
    return pl.CostEstimate(flops=cost * 2**20, bytes_accessed=0, transcendentals=0)


def params():
    return pltpu.CompilerParams(vmem_limit_bytes=VMEM_BYTES)


def rope_tables(length, width):
    inverse = ROPE_BASE ** (np.arange(width // 2) * (-2.0 / width))
    angles = np.arange(length)[:, None] * inverse[None, :]
    cosine, sine = np.cos(angles), np.sin(angles)
    cosine, sine = np.concatenate([cosine, cosine], 1), np.concatenate([-sine, sine], 1)
    return jnp.asarray(cosine, jnp.float32), jnp.asarray(sine, jnp.float32)


ANY = pl.BlockSpec(memory_space=pl.ANY)


def combine_kernel(shares, near, far, *rest):
    out = rest[-1]
    mixed = shares[0] * near[...].astype(jnp.float32) + shares[1] * far[...].astype(jnp.float32)
    out[...] = mixed.astype(out.dtype)


def combine(shares, near, far, near_block, width, after=(), cost=0):
    rows, columns = far.shape
    step = min(rows, 512)
    block = pl.BlockSpec((step, width), lambda i, j: (i, j))
    return pl.pallas_call(
        combine_kernel,
        out_shape=jax.ShapeDtypeStruct(far.shape, far.dtype),
        grid=(rows // step, columns // width),
        in_specs=[SMEM, pl.BlockSpec((step, width), lambda i, j: (i, near_block(j))), block]
        + [ANY] * len(after),
        out_specs=block,
        compiler_params=params(),
        cost_estimate=estimate(cost),
    )(shares, near, far, *after)


def columns_kernel(whole, *rest):
    rest[-1][...] = whole[...]


def columns_of(whole, block, width, pieces, after=(), cost=0):
    rows = whole.shape[0]
    step = min(rows, 512)
    return pl.pallas_call(
        columns_kernel,
        out_shape=jax.ShapeDtypeStruct((rows, pieces * width), whole.dtype),
        grid=(rows // step, pieces),
        in_specs=[pl.BlockSpec((step, width), lambda i, j: (i, block(j)))] + [ANY] * len(after),
        out_specs=pl.BlockSpec((step, width), lambda i, j: (i, j)),
        compiler_params=params(),
        cost_estimate=estimate(cost),
    )(whole, *after)


def copy_kernel(source, *rest):
    rest[-1][...] = source[...]


def copied(array, after, cost=0):
    return pl.pallas_call(
        copy_kernel,
        out_shape=jax.ShapeDtypeStruct(array.shape, array.dtype),
        in_specs=[VMEM] + [ANY] * len(after),
        out_specs=VMEM,
        compiler_params=params(),
        cost_estimate=estimate(cost),
    )(array, *after)


def project(ids, blocks, own, other, whole):
    half = own.shape[0]
    mine, place, count = ids[0], ids[1], len(blocks)
    whole[pl.ds(pl.multiple_of(mine * half, half), half), :] = own[...]
    whole[pl.ds(pl.multiple_of((1 - mine) * half, half), half), :] = other[...]
    total = None
    for k, block in enumerate(blocks):
        width = block.shape[1]
        owner = lax.rem(place - k + count, count)
        rows = pl.ds(pl.multiple_of(owner * width, width), width)
        term = jnp.dot(block[...], whole[rows, :], preferred_element_type=jnp.float32)
        total = term if total is None else total + term
    return total


def norm_rope(vectors, cosine, signed_sine):
    meansq = jnp.mean(vectors * vectors, axis=-1, keepdims=True)
    normed = vectors * lax.rsqrt(meansq + EPSILON)
    return normed * cosine + pltpu.roll(normed, HEAD_DIM // 2, 1) * signed_sine


def keyval_kernel(count, ids, *refs):
    blocks = refs[:count]
    own, other, cosine, sine = refs[count : count + 4]
    keys, values, scales, whole = refs[-4:]
    total = 0.0
    features = 0
    for block in blocks:
        rows = block[...].astype(jnp.float32)
        total = total + jnp.sum(rows * rows, axis=-1, keepdims=True)
        features += block.shape[1]
    scale = lax.rsqrt(total / features + EPSILON)
    raw = project(ids, blocks, own, other, whole) * scale
    keys[...] = norm_rope(raw[:, :HEAD_DIM], cosine[...], sine[...]).astype(keys.dtype)
    values[...] = raw[:, HEAD_DIM:].astype(values.dtype)
    scales[...] = jnp.broadcast_to(scale, scales.shape)


def keyval(ids, blocks, own, other, cosine, sine, after=(), cost=0):
    length = blocks[0].shape[0]
    features = sum(b.shape[1] for b in blocks)
    head = jax.ShapeDtypeStruct((length, HEAD_DIM), jnp.bfloat16)
    return pl.pallas_call(
        functools.partial(keyval_kernel, len(blocks)),
        out_shape=(head, head, jax.ShapeDtypeStruct((length, LANES), jnp.float32)),
        in_specs=[SMEM] + [VMEM] * (len(blocks) + 4) + [ANY] * len(after),
        out_specs=(VMEM,) * 3,
        scratch_shapes=[pltpu.VMEM((features, own.shape[1]), own.dtype)],
        compiler_params=params(),
        cost_estimate=estimate(cost),
    )(ids, *blocks, own, other, cosine, sine, *after)


def attend_kernel(count, ids, *refs):
    blocks = refs[:count]
    own, other, keys, values, scales, cosine, sine = refs[count : count + 7]
    mixed, whole = refs[-2:]
    raw = project(ids, blocks, own, other, whole)
    length = raw.shape[0]
    rows = length // 2 if length % 16 == 0 else length
    scale = scales[:, :1]
    for head in range(raw.shape[1] // HEAD_DIM):
        columns = slice(head * HEAD_DIM, (head + 1) * HEAD_DIM)
        query = norm_rope(raw[:, columns] * scale, cosine[...], sine[...]).astype(jnp.bfloat16)
        for first in range(0, length, rows):
            last = first + rows
            scores = lax.dot_general(
                query[first:last],
                keys[:last, :],
                (((1,), (1,)), ((), ())),
                preferred_element_type=jnp.float32,
            )
            expo = jnp.exp(scores * (1.0 / math.sqrt(HEAD_DIM)) - math.sqrt(HEAD_DIM))
            at = first + lax.broadcasted_iota(jnp.int32, expo.shape, 0)
            expo = jnp.where(lax.broadcasted_iota(jnp.int32, expo.shape, 1) <= at, expo, 0.0)
            total = jnp.sum(expo, axis=-1, keepdims=True)
            product = jnp.dot(
                expo.astype(jnp.bfloat16), values[:last, :], preferred_element_type=jnp.float32
            )
            mixed[first:last, columns] = (product / total).astype(mixed.dtype)


def attend(ids, blocks, own, other, keys, values, scales, cosine, sine, after=(), cost=0):
    length = blocks[0].shape[0]
    features = sum(b.shape[1] for b in blocks)
    width = own.shape[1]
    return pl.pallas_call(
        functools.partial(attend_kernel, len(blocks)),
        out_shape=jax.ShapeDtypeStruct((length, width), jnp.bfloat16),
        in_specs=[SMEM] + [VMEM] * (len(blocks) + 7) + [ANY] * len(after),
        out_specs=VMEM,
        scratch_shapes=[pltpu.VMEM((features, width), own.dtype)],
        compiler_params=params(),
        cost_estimate=estimate(cost),
    )(ids, *blocks, own, other, keys, values, scales, cosine, sine, *after)


def products(ids, mixed, own, other, by_owner):
    mine = ids[0]
    count, _, width = by_owner.shape
    per_half = count // 2
    for half, weights in ((mine, own), (1 - mine, other)):
        total = None
        depth = 0
        for part in mixed:
            rows = slice(depth, depth + part.shape[1])
            depth += part.shape[1]
            term = jnp.dot(part[...], weights[rows, :], preferred_element_type=jnp.float32)
            total = term if total is None else total + term
        for piece in range(per_half):
            by_owner[half * per_half + piece] = total[
                :, piece * width : (piece + 1) * width
            ].astype(by_owner.dtype)


def partial_kernel(count, parts, ids, *refs):
    kept, sent, by_owner = refs[-3:]
    products(ids, refs[:parts], refs[parts], refs[parts + 1], by_owner)
    low = lax.rem(ids[1], 2)
    for pair in range(count // 2):
        kept[pair] = by_owner[2 * pair + low]
        sent[pair] = by_owner[2 * pair + 1 - low]


def direct_kernel(count, parts, ids, *refs):
    outs, by_owner = refs[-1 - count : -1], refs[-1]
    products(ids, refs[:parts], refs[parts], refs[parts + 1], by_owner)
    for k in range(count):
        outs[k][...] = by_owner[lax.rem(ids[1] + k, count)]


def direct_partials(ids, mixed, own, other, count, after=(), cost=0):
    length = mixed[0].shape[0]
    width = 2 * own.shape[1] // count
    piece = jax.ShapeDtypeStruct((length, width), jnp.bfloat16)
    return pl.pallas_call(
        functools.partial(direct_kernel, count, len(mixed)),
        out_shape=(piece,) * count,
        in_specs=[SMEM] + [VMEM] * (len(mixed) + 2) + [ANY] * len(after),
        out_specs=(VMEM,) * count,
        scratch_shapes=[pltpu.VMEM((count, length, width), jnp.bfloat16)],
        compiler_params=params(),
        cost_estimate=estimate(cost),
    )(ids, *mixed, own, other, *after)


def partials(ids, mixed, own, other, count, after=(), cost=0):
    length = mixed[0].shape[0]
    width = 2 * own.shape[1] // count
    half = jax.ShapeDtypeStruct((count // 2, length, width), jnp.bfloat16)
    return pl.pallas_call(
        functools.partial(partial_kernel, count, len(mixed)),
        out_shape=(half, half),
        in_specs=[SMEM] + [VMEM] * (len(mixed) + 2) + [ANY] * len(after),
        out_specs=(VMEM, VMEM),
        scratch_shapes=[pltpu.VMEM((count, length, width), jnp.bfloat16)],
        compiler_params=params(),
        cost_estimate=estimate(cost),
    )(ids, *mixed, own, other, *after)


def reduce_kernel(ids, kept, got, *refs):
    still, sent = refs[-2:]
    high = lax.rem(lax.div(ids[1], 2), 2)
    still[...] = kept[high].astype(jnp.float32) + got[high].astype(jnp.float32)
    away = kept[1 - high].astype(jnp.float32) + got[1 - high].astype(jnp.float32)
    sent[...] = away.astype(sent.dtype)


def reduce(ids, kept, got, after=(), cost=0):
    shape = kept.shape[1:]
    return pl.pallas_call(
        reduce_kernel,
        out_shape=(
            jax.ShapeDtypeStruct(shape, jnp.float32),
            jax.ShapeDtypeStruct(shape, jnp.bfloat16),
        ),
        in_specs=[SMEM, VMEM, VMEM] + [ANY] * len(after),
        out_specs=(VMEM, VMEM),
        compiler_params=params(),
        cost_estimate=estimate(cost),
    )(ids, kept, got, *after)


def leave_kernel(counts, rows, *refs):
    out = refs[-1]
    width = rows.shape[1] // len(counts)
    first = 0
    for chunk, count in enumerate(counts):
        columns = slice(chunk * width, (chunk + 1) * width)
        total = rows[:, columns].astype(jnp.float32)
        for piece in refs[first : first + count]:
            total = total + piece[...].astype(jnp.float32)
        first += count
        out[:, columns] = total.astype(out.dtype)


def leave(rows, pieces):
    flat = [piece for chunk in pieces for piece in chunk]
    return pl.pallas_call(
        functools.partial(leave_kernel, [len(chunk) for chunk in pieces]),
        out_shape=jax.ShapeDtypeStruct(rows.shape, rows.dtype),
        in_specs=[VMEM] * (1 + len(flat)),
        out_specs=VMEM,
        compiler_params=params(),
        cost_estimate=estimate(1),
    )(rows, *flat)


def permute(array, axis, source):
    count = lax.axis_size(axis)
    return lax.ppermute(array, axis, [(source(i) % count, i) for i in range(count)])


def from_near(array):
    return permute(array, "section", lambda i: i ^ 1)


def from_far(array):
    return permute(array, "section", lambda i: i + 1 if i % 2 else i - 1)


def from_other_half(array):
    return permute(array, "fsdp", lambda i: i ^ 1)


def body(entering, w_query, w_keyval, w_out):
    count = lax.axis_size("tensor")
    section = lax.axis_index("section")
    ids = jnp.stack([lax.axis_index("fsdp"), lax.axis_index("tensor")]).astype(jnp.int32)
    shares = jnp.where(
        section % 2 == 0,
        jnp.array([AFTER_SHARE, BEFORE_SHARE], jnp.float32),
        jnp.array([BEFORE_SHARE, AFTER_SHARE], jnp.float32),
    )
    rows = entering[0]
    length = rows.shape[0]
    own_query = w_query[0]
    own_keyval = w_keyval.reshape(w_keyval.shape[1], -1)
    own_out = w_out[0]
    query_width = own_query.shape[1] // QUERY_CHUNKS
    halves = count // 2
    quarter = own_out.shape[1] // halves
    out_width = quarter // OUT_CHUNKS

    near_keyval, near_query, near_out = map(from_near, (own_keyval, own_query, own_out))
    far = {0: from_far(own_keyval)}
    places = [(own_keyval, near_keyval, own_keyval.shape[1], lambda j: 0)]
    for c in range(QUERY_CHUNKS):
        places.append((own_query, near_query, query_width, lambda j, c=c: c))
    for c in range(OUT_CHUNKS):
        places.append((own_out, near_out, out_width, lambda j, c=c: j * OUT_CHUNKS + c))
    pieces_of = [1] * (1 + QUERY_CHUNKS) + [halves] * OUT_CHUNKS
    blocks = [rows] + [None] * (count - 1)
    for k in FIRST:
        blocks[k] = permute(rows, "tensor", lambda i, k=k: i - k)
    cosine, sine = rope_tables(length, HEAD_DIM)

    own, other, mixed, halves_of, pieces, before = {}, {}, [], {}, {}, []
    for kind, c, arrivals, cost in STEPS:
        after = list(before)
        for name in arrivals.split():
            if name[0] == "y":
                after.append(other[int(name[1:])])
            elif name[0] == "a":
                after.append(blocks[int(name[1:])])
            elif name[0] == "n":
                after.append((near_query, near_out)[int(name[1:])])
            elif name[0] == "s":
                after.append(halves_of[int(name[1:])][1])
            else:
                after.append(pieces[int(name[1:])][1])
        if kind == "G":
            whole, _, width, place = places[c]
            chunk = columns_of(whole, place, width, pieces_of[c], after=after, cost=cost)
            far[c] = from_far(chunk)
            before = [chunk]
        elif kind == "C":
            _, near, width, place = places[c]
            own[c] = combine(shares, near, far[c], place, width, after=after, cost=cost)
            other[c] = from_other_half(own[c])
            before = [own[c]]
        elif kind == "X":
            again = copied(rows, after=after + [blocks[k] for k in FIRST], cost=cost)
            for k in range(1, count):
                if k not in FIRST:
                    blocks[k] = permute(again, "tensor", lambda i, k=k: i - k)
            before = [again]
        elif kind == "K":
            keys, values, scales = keyval(
                ids, blocks, own[c], other[c], cosine, sine, after=after, cost=cost
            )
            before = [scales]
        elif kind == "A":
            mixed.append(
                attend(
                    ids,
                    blocks,
                    own[c],
                    other[c],
                    keys,
                    values,
                    scales,
                    cosine,
                    sine,
                    after=after,
                    cost=cost,
                )
            )
            before = [mixed[-1]]
        elif kind == "P":
            kept, sent = partials(
                ids, mixed, own[c], other[c], count, after=after, cost=cost
            )
            halves_of[c] = (kept, permute(sent, "tensor", lambda i: i ^ 1))
            before = [kept]
        elif kind == "Q":
            parts = direct_partials(
                ids, mixed, own[c], other[c], count, after=after, cost=cost
            )
            pieces[c] = [parts[0]] + [
                permute(parts[k], "tensor", lambda i, k=k: i - k) for k in range(1, count)
            ]
            before = [parts[0]]
        else:
            kept, sent = reduce(ids, *halves_of[c], after=after, cost=cost)
            pieces[c] = (kept, permute(sent, "tensor", lambda i: i ^ 2))
            before = [kept]
    pieces = [pieces[c] for c in sorted(pieces)]
    return leave(rows, pieces)[None]


def shifted(block, axis, distance):
    return permute(block, axis, lambda i: i - distance)


def head_norm_rope(vectors, cosine, signed_sine):
    meansq = jnp.mean(vectors * vectors, axis=-1, keepdims=True)
    normed = vectors * lax.rsqrt(meansq + EPSILON)
    return normed * cosine + jnp.roll(normed, vectors.shape[-1] // 2, axis=-1) * signed_sine


def rebuilt(weights):
    before = shifted(weights, "section", 1).astype(jnp.float32)
    after = shifted(weights, "section", -1).astype(jnp.float32)
    return (BEFORE_SHARE * before + AFTER_SHARE * after).astype(jnp.bfloat16)


def general_body(entering, w_query, w_keyval, w_out):
    rows = entering[0].astype(jnp.float32)
    features = rows.shape[1] * lax.axis_size("tensor")
    square_total = lax.psum(jnp.sum(rows * rows, axis=-1, keepdims=True), "tensor")
    normed = (rows * lax.rsqrt(square_total / features + EPSILON)).astype(jnp.bfloat16)
    normed = lax.all_gather(normed, "tensor", axis=1, tiled=True)
    length = normed.shape[0]
    query_weight = lax.all_gather(rebuilt(w_query)[0], "fsdp", axis=0, tiled=True)
    keyval_weight = lax.all_gather(rebuilt(w_keyval)[0], "fsdp", axis=0, tiled=True)
    out_weight = lax.all_gather(rebuilt(w_out)[0], "fsdp", axis=1, tiled=True)
    kv_count = keyval_weight.shape[1]
    raw = jnp.dot(normed, query_weight, preferred_element_type=jnp.float32)
    raw = raw.reshape(length, kv_count, -1, HEAD_DIM)
    keyval_raw = jnp.dot(
        normed, keyval_weight.reshape(features, -1), preferred_element_type=jnp.float32
    ).reshape(length, kv_count, 2 * HEAD_DIM)
    cosine, sine = rope_tables(length, HEAD_DIM)
    queries = head_norm_rope(raw, cosine[:, None, None], sine[:, None, None]).astype(jnp.bfloat16)
    keys = head_norm_rope(
        keyval_raw[..., :HEAD_DIM], cosine[:, None], sine[:, None]
    ).astype(jnp.bfloat16)
    values = keyval_raw[..., HEAD_DIM:].astype(jnp.bfloat16)
    causal = jnp.arange(length)[:, None] >= jnp.arange(length)[None, :]

    def one_group(query_slice):
        scores = jnp.einsum("qkd,pkd->kqp", query_slice, keys, preferred_element_type=jnp.float32)
        expo = jnp.exp(scores * (1.0 / math.sqrt(HEAD_DIM)) - math.sqrt(HEAD_DIM))
        expo = jnp.where(causal[None], expo, 0.0)
        weights = (expo / jnp.sum(expo, axis=-1, keepdims=True)).astype(jnp.bfloat16)
        return jnp.einsum(
            "kqp,pkd->qkd", weights, values, preferred_element_type=jnp.float32
        ).astype(jnp.bfloat16)

    mixed = lax.map(one_group, jnp.moveaxis(queries, 2, 0))
    mixed = jnp.moveaxis(mixed, 0, 2).reshape(length, -1)
    terms = jnp.dot(mixed, out_weight, preferred_element_type=jnp.float32).astype(jnp.bfloat16)
    summed = lax.psum_scatter(terms, "tensor", scatter_dimension=1, tiled=True)
    return (rows + summed.astype(jnp.float32)).astype(jnp.bfloat16)[None]


def solution(mesh):
    in_specs = (
        P("section", "fsdp", "tensor"),
        P("section", "fsdp", "tensor"),
        P("section", "fsdp", "tensor", None),
        P("section", "tensor", "fsdp"),
    )
    out_specs = P("section", "fsdp", "tensor")

    def step(entering, w_query, w_keyval, w_out):
        chunked = (
            mesh.shape["section"] % 2 == 0
            and mesh.shape["fsdp"] == 2
            and mesh.shape["tensor"] == 4
            and w_keyval.shape[2] == mesh.shape["tensor"]
            and w_keyval.shape[3] == 2 * HEAD_DIM
            and w_query.shape[2] % (mesh.shape["tensor"] * QUERY_CHUNKS * HEAD_DIM) == 0
            and w_out.shape[2] % (mesh.shape["tensor"] * OUT_CHUNKS * LANES) == 0
        )
        return jax.shard_map(
            body if chunked else general_body,
            mesh=mesh,
            in_specs=in_specs,
            out_specs=out_specs,
            check_vma=False,
        )(entering, w_query, w_keyval, w_out)

    return step
```

```python
import functools
import math

import jax
import jax.numpy as jnp
import numpy as np
from jax import lax
from jax.experimental import pallas as pl
from jax.experimental.pallas import tpu as pltpu
from jax.sharding import PartitionSpec as P

HEAD_DIM = 128
EPSILON = 1e-06
ROPE_BASE = 1000000.0
BEFORE_SHARE = 0.6
AFTER_SHARE = 0.4
LANES = 128
VMEM_BYTES = 48 * 1024 * 1024
QUERY_CHUNKS = 4
OUT_CHUNKS = 4
FIRST = (1, 3)
STEPS = (('G', 1, 'n1', 6000), ('G', 2, '', 6000), ('C', 0, '', 700), ('G', 3, '', 6000), ('C', 1, '', 4000), ('X', 0, '', 200), ('G', 4, '', 6000), ('C', 2, '', 0), ('G', 5, 'y0', 6000), ('C', 3, 'y1', 4000), ('K', 0, '', 6000), ('G', 6, '', 6000), ('C', 4, '', 0), ('A', 1, 'a1', 0), ('A', 2, 'a3', 2000), ('A', 3, '', 1000), ('C', 5, '', 4000), ('A', 4, '', 2000), ('G', 8, '', 6000), ('G', 7, '', 6000), ('C', 6, '', 0), ('P', 5, '', 3000), ('C', 7, '', 4000), ('R', 5, 'y3', 1000), ('P', 6, '', 6000), ('C', 8, '', 0), ('P', 7, 't5', 3000), ('R', 6, 'y4', 50), ('R', 7, '', 1000), ('Q', 8, 'a2', 4000))

SMEM = pl.BlockSpec(memory_space=pltpu.SMEM)
VMEM = pl.BlockSpec(memory_space=pltpu.VMEM)


def estimate(cost):
    return pl.CostEstimate(flops=cost * 2**20, bytes_accessed=0, transcendentals=0)


def params():
    return pltpu.CompilerParams(vmem_limit_bytes=VMEM_BYTES)


def rope_tables(length, width):
    inverse = ROPE_BASE ** (np.arange(width // 2) * (-2.0 / width))
    angles = np.arange(length)[:, None] * inverse[None, :]
    cosine, sine = np.cos(angles), np.sin(angles)
    cosine, sine = np.concatenate([cosine, cosine], 1), np.concatenate([-sine, sine], 1)
    return jnp.asarray(cosine, jnp.float32), jnp.asarray(sine, jnp.float32)


ANY = pl.BlockSpec(memory_space=pl.ANY)


def combine_kernel(shares, near, far, *rest):
    out = rest[-1]
    mixed = shares[0] * near[...].astype(jnp.float32) + shares[1] * far[...].astype(jnp.float32)
    out[...] = mixed.astype(out.dtype)


def combine(shares, near, far, near_block, width, after=(), cost=0):
    rows, columns = far.shape
    step = min(rows, 512)
    block = pl.BlockSpec((step, width), lambda i, j: (i, j))
    return pl.pallas_call(
        combine_kernel,
        out_shape=jax.ShapeDtypeStruct(far.shape, far.dtype),
        grid=(rows // step, columns // width),
        in_specs=[SMEM, pl.BlockSpec((step, width), lambda i, j: (i, near_block(j))), block]
        + [ANY] * len(after),
        out_specs=block,
        compiler_params=params(),
        cost_estimate=estimate(cost),
    )(shares, near, far, *after)


def columns_kernel(whole, *rest):
    rest[-1][...] = whole[...]


def columns_of(whole, block, width, pieces, after=(), cost=0):
    rows = whole.shape[0]
    step = min(rows, 512)
    return pl.pallas_call(
        columns_kernel,
        out_shape=jax.ShapeDtypeStruct((rows, pieces * width), whole.dtype),
        grid=(rows // step, pieces),
        in_specs=[pl.BlockSpec((step, width), lambda i, j: (i, block(j)))] + [ANY] * len(after),
        out_specs=pl.BlockSpec((step, width), lambda i, j: (i, j)),
        compiler_params=params(),
        cost_estimate=estimate(cost),
    )(whole, *after)


def copy_kernel(source, *rest):
    rest[-1][...] = source[...]


def copied(array, after, cost=0):
    return pl.pallas_call(
        copy_kernel,
        out_shape=jax.ShapeDtypeStruct(array.shape, array.dtype),
        in_specs=[VMEM] + [ANY] * len(after),
        out_specs=VMEM,
        compiler_params=params(),
        cost_estimate=estimate(cost),
    )(array, *after)


def project(ids, blocks, own, other, whole):
    half = own.shape[0]
    mine, place, count = ids[0], ids[1], len(blocks)
    whole[pl.ds(pl.multiple_of(mine * half, half), half), :] = own[...]
    whole[pl.ds(pl.multiple_of((1 - mine) * half, half), half), :] = other[...]
    total = None
    for k, block in enumerate(blocks):
        width = block.shape[1]
        owner = lax.rem(place - k + count, count)
        rows = pl.ds(pl.multiple_of(owner * width, width), width)
        term = jnp.dot(block[...], whole[rows, :], preferred_element_type=jnp.float32)
        total = term if total is None else total + term
    return total


def norm_rope(vectors, cosine, signed_sine):
    meansq = jnp.mean(vectors * vectors, axis=-1, keepdims=True)
    normed = vectors * lax.rsqrt(meansq + EPSILON)
    return normed * cosine + pltpu.roll(normed, HEAD_DIM // 2, 1) * signed_sine


def keyval_kernel(count, ids, *refs):
    blocks = refs[:count]
    own, other, cosine, sine = refs[count : count + 4]
    keys, values, scales, whole = refs[-4:]
    total = 0.0
    features = 0
    for block in blocks:
        rows = block[...].astype(jnp.float32)
        total = total + jnp.sum(rows * rows, axis=-1, keepdims=True)
        features += block.shape[1]
    scale = lax.rsqrt(total / features + EPSILON)
    raw = project(ids, blocks, own, other, whole) * scale
    keys[...] = norm_rope(raw[:, :HEAD_DIM], cosine[...], sine[...]).astype(keys.dtype)
    values[...] = raw[:, HEAD_DIM:].astype(values.dtype)
    scales[...] = jnp.broadcast_to(scale, scales.shape)


def keyval(ids, blocks, own, other, cosine, sine, after=(), cost=0):
    length = blocks[0].shape[0]
    features = sum(b.shape[1] for b in blocks)
    head = jax.ShapeDtypeStruct((length, HEAD_DIM), jnp.bfloat16)
    return pl.pallas_call(
        functools.partial(keyval_kernel, len(blocks)),
        out_shape=(head, head, jax.ShapeDtypeStruct((length, LANES), jnp.float32)),
        in_specs=[SMEM] + [VMEM] * (len(blocks) + 4) + [ANY] * len(after),
        out_specs=(VMEM,) * 3,
        scratch_shapes=[pltpu.VMEM((features, own.shape[1]), own.dtype)],
        compiler_params=params(),
        cost_estimate=estimate(cost),
    )(ids, *blocks, own, other, cosine, sine, *after)


def attend_kernel(count, ids, *refs):
    blocks = refs[:count]
    own, other, keys, values, scales, cosine, sine = refs[count : count + 7]
    mixed, whole = refs[-2:]
    raw = project(ids, blocks, own, other, whole)
    length = raw.shape[0]
    rows = length // 2 if length % 16 == 0 else length
    scale = scales[:, :1]
    for head in range(raw.shape[1] // HEAD_DIM):
        columns = slice(head * HEAD_DIM, (head + 1) * HEAD_DIM)
        query = norm_rope(raw[:, columns] * scale, cosine[...], sine[...]).astype(jnp.bfloat16)
        for first in range(0, length, rows):
            last = first + rows
            scores = lax.dot_general(
                query[first:last],
                keys[:last, :],
                (((1,), (1,)), ((), ())),
                preferred_element_type=jnp.float32,
            )
            expo = jnp.exp(scores * (1.0 / math.sqrt(HEAD_DIM)) - math.sqrt(HEAD_DIM))
            at = first + lax.broadcasted_iota(jnp.int32, expo.shape, 0)
            expo = jnp.where(lax.broadcasted_iota(jnp.int32, expo.shape, 1) <= at, expo, 0.0)
            total = jnp.sum(expo, axis=-1, keepdims=True)
            product = jnp.dot(
                expo.astype(jnp.bfloat16), values[:last, :], preferred_element_type=jnp.float32
            )
            mixed[first:last, columns] = (product / total).astype(mixed.dtype)


def attend(ids, blocks, own, other, keys, values, scales, cosine, sine, after=(), cost=0):
    length = blocks[0].shape[0]
    features = sum(b.shape[1] for b in blocks)
    width = own.shape[1]
    return pl.pallas_call(
        functools.partial(attend_kernel, len(blocks)),
        out_shape=jax.ShapeDtypeStruct((length, width), jnp.bfloat16),
        in_specs=[SMEM] + [VMEM] * (len(blocks) + 7) + [ANY] * len(after),
        out_specs=VMEM,
        scratch_shapes=[pltpu.VMEM((features, width), own.dtype)],
        compiler_params=params(),
        cost_estimate=estimate(cost),
    )(ids, *blocks, own, other, keys, values, scales, cosine, sine, *after)


def products(ids, mixed, own, other, by_owner):
    mine = ids[0]
    count, _, width = by_owner.shape
    per_half = count // 2
    for half, weights in ((mine, own), (1 - mine, other)):
        total = None
        depth = 0
        for part in mixed:
            rows = slice(depth, depth + part.shape[1])
            depth += part.shape[1]
            term = jnp.dot(part[...], weights[rows, :], preferred_element_type=jnp.float32)
            total = term if total is None else total + term
        for piece in range(per_half):
            by_owner[half * per_half + piece] = total[
                :, piece * width : (piece + 1) * width
            ].astype(by_owner.dtype)


def partial_kernel(count, parts, ids, *refs):
    kept, sent, by_owner = refs[-3:]
    products(ids, refs[:parts], refs[parts], refs[parts + 1], by_owner)
    low = lax.rem(ids[1], 2)
    for pair in range(count // 2):
        kept[pair] = by_owner[2 * pair + low]
        sent[pair] = by_owner[2 * pair + 1 - low]


def direct_kernel(count, parts, ids, *refs):
    outs, by_owner = refs[-1 - count : -1], refs[-1]
    products(ids, refs[:parts], refs[parts], refs[parts + 1], by_owner)
    for k in range(count):
        outs[k][...] = by_owner[lax.rem(ids[1] + k, count)]


def direct_partials(ids, mixed, own, other, count, after=(), cost=0):
    length = mixed[0].shape[0]
    width = 2 * own.shape[1] // count
    piece = jax.ShapeDtypeStruct((length, width), jnp.bfloat16)
    return pl.pallas_call(
        functools.partial(direct_kernel, count, len(mixed)),
        out_shape=(piece,) * count,
        in_specs=[SMEM] + [VMEM] * (len(mixed) + 2) + [ANY] * len(after),
        out_specs=(VMEM,) * count,
        scratch_shapes=[pltpu.VMEM((count, length, width), jnp.bfloat16)],
        compiler_params=params(),
        cost_estimate=estimate(cost),
    )(ids, *mixed, own, other, *after)


def partials(ids, mixed, own, other, count, after=(), cost=0):
    length = mixed[0].shape[0]
    width = 2 * own.shape[1] // count
    half = jax.ShapeDtypeStruct((count // 2, length, width), jnp.bfloat16)
    return pl.pallas_call(
        functools.partial(partial_kernel, count, len(mixed)),
        out_shape=(half, half),
        in_specs=[SMEM] + [VMEM] * (len(mixed) + 2) + [ANY] * len(after),
        out_specs=(VMEM, VMEM),
        scratch_shapes=[pltpu.VMEM((count, length, width), jnp.bfloat16)],
        compiler_params=params(),
        cost_estimate=estimate(cost),
    )(ids, *mixed, own, other, *after)


def reduce_kernel(ids, kept, got, *refs):
    still, sent = refs[-2:]
    high = lax.rem(lax.div(ids[1], 2), 2)
    still[...] = kept[high].astype(jnp.float32) + got[high].astype(jnp.float32)
    away = kept[1 - high].astype(jnp.float32) + got[1 - high].astype(jnp.float32)
    sent[...] = away.astype(sent.dtype)


def reduce(ids, kept, got, after=(), cost=0):
    shape = kept.shape[1:]
    return pl.pallas_call(
        reduce_kernel,
        out_shape=(
            jax.ShapeDtypeStruct(shape, jnp.float32),
            jax.ShapeDtypeStruct(shape, jnp.bfloat16),
        ),
        in_specs=[SMEM, VMEM, VMEM] + [ANY] * len(after),
        out_specs=(VMEM, VMEM),
        compiler_params=params(),
        cost_estimate=estimate(cost),
    )(ids, kept, got, *after)


def leave_kernel(counts, rows, *refs):
    out = refs[-1]
    width = rows.shape[1] // len(counts)
    first = 0
    for chunk, count in enumerate(counts):
        columns = slice(chunk * width, (chunk + 1) * width)
        total = rows[:, columns].astype(jnp.float32)
        for piece in refs[first : first + count]:
            total = total + piece[...].astype(jnp.float32)
        first += count
        out[:, columns] = total.astype(out.dtype)


def leave(rows, pieces):
    flat = [piece for chunk in pieces for piece in chunk]
    return pl.pallas_call(
        functools.partial(leave_kernel, [len(chunk) for chunk in pieces]),
        out_shape=jax.ShapeDtypeStruct(rows.shape, rows.dtype),
        in_specs=[VMEM] * (1 + len(flat)),
        out_specs=VMEM,
        compiler_params=params(),
        cost_estimate=estimate(1),
    )(rows, *flat)


def permute(array, axis, source):
    count = lax.axis_size(axis)
    return lax.ppermute(array, axis, [(source(i) % count, i) for i in range(count)])


def from_near(array):
    return permute(array, "section", lambda i: i ^ 1)


def from_far(array):
    return permute(array, "section", lambda i: i + 1 if i % 2 else i - 1)


def from_other_half(array):
    return permute(array, "fsdp", lambda i: i ^ 1)


def body(entering, w_query, w_keyval, w_out):
    count = lax.axis_size("tensor")
    section = lax.axis_index("section")
    ids = jnp.stack([lax.axis_index("fsdp"), lax.axis_index("tensor")]).astype(jnp.int32)
    shares = jnp.where(
        section % 2 == 0,
        jnp.array([AFTER_SHARE, BEFORE_SHARE], jnp.float32),
        jnp.array([BEFORE_SHARE, AFTER_SHARE], jnp.float32),
    )
    rows = entering[0]
    length = rows.shape[0]
    own_query = w_query[0]
    own_keyval = w_keyval.reshape(w_keyval.shape[1], -1)
    own_out = w_out[0]
    query_width = own_query.shape[1] // QUERY_CHUNKS
    halves = count // 2
    quarter = own_out.shape[1] // halves
    out_width = quarter // OUT_CHUNKS

    near_keyval, near_query, near_out = map(from_near, (own_keyval, own_query, own_out))
    far = {0: from_far(own_keyval)}
    places = [(own_keyval, near_keyval, own_keyval.shape[1], lambda j: 0)]
    for c in range(QUERY_CHUNKS):
        places.append((own_query, near_query, query_width, lambda j, c=c: c))
    for c in range(OUT_CHUNKS):
        places.append((own_out, near_out, out_width, lambda j, c=c: j * OUT_CHUNKS + c))
    pieces_of = [1] * (1 + QUERY_CHUNKS) + [halves] * OUT_CHUNKS
    blocks = [rows] + [None] * (count - 1)
    for k in FIRST:
        blocks[k] = permute(rows, "tensor", lambda i, k=k: i - k)
    cosine, sine = rope_tables(length, HEAD_DIM)

    own, other, mixed, halves_of, pieces, before = {}, {}, [], {}, {}, []
    for kind, c, arrivals, cost in STEPS:
        after = list(before)
        for name in arrivals.split():
            if name[0] == "y":
                after.append(other[int(name[1:])])
            elif name[0] == "a":
                after.append(blocks[int(name[1:])])
            elif name[0] == "n":
                after.append((near_query, near_out)[int(name[1:])])
            elif name[0] == "s":
                after.append(halves_of[int(name[1:])][1])
            else:
                after.append(pieces[int(name[1:])][1])
        if kind == "G":
            whole, _, width, place = places[c]
            chunk = columns_of(whole, place, width, pieces_of[c], after=after, cost=cost)
            far[c] = from_far(chunk)
            before = [chunk]
        elif kind == "C":
            _, near, width, place = places[c]
            own[c] = combine(shares, near, far[c], place, width, after=after, cost=cost)
            other[c] = from_other_half(own[c])
            before = [own[c]]
        elif kind == "X":
            again = copied(rows, after=after + [blocks[k] for k in FIRST], cost=cost)
            for k in range(1, count):
                if k not in FIRST:
                    blocks[k] = permute(again, "tensor", lambda i, k=k: i - k)
            before = [again]
        elif kind == "K":
            keys, values, scales = keyval(
                ids, blocks, own[c], other[c], cosine, sine, after=after, cost=cost
            )
            before = [scales]
        elif kind == "A":
            mixed.append(
                attend(
                    ids,
                    blocks,
                    own[c],
                    other[c],
                    keys,
                    values,
                    scales,
                    cosine,
                    sine,
                    after=after,
                    cost=cost,
                )
            )
            before = [mixed[-1]]
        elif kind == "P":
            kept, sent = partials(
                ids, mixed, own[c], other[c], count, after=after, cost=cost
            )
            halves_of[c] = (kept, permute(sent, "tensor", lambda i: i ^ 1))
            before = [kept]
        elif kind == "Q":
            parts = direct_partials(
                ids, mixed, own[c], other[c], count, after=after, cost=cost
            )
            pieces[c] = [parts[0]] + [
                permute(parts[k], "tensor", lambda i, k=k: i - k) for k in sorted(range(1, count), key=lambda k: -min(k, count - k))
            ]
            before = [parts[0]]
        else:
            kept, sent = reduce(ids, *halves_of[c], after=after, cost=cost)
            pieces[c] = (kept, permute(sent, "tensor", lambda i: i ^ 2))
            before = [kept]
    pieces = [pieces[c] for c in sorted(pieces)]
    return leave(rows, pieces)[None]


def shifted(block, axis, distance):
    return permute(block, axis, lambda i: i - distance)


def head_norm_rope(vectors, cosine, signed_sine):
    meansq = jnp.mean(vectors * vectors, axis=-1, keepdims=True)
    normed = vectors * lax.rsqrt(meansq + EPSILON)
    return normed * cosine + jnp.roll(normed, vectors.shape[-1] // 2, axis=-1) * signed_sine


def rebuilt(weights):
    before = shifted(weights, "section", 1).astype(jnp.float32)
    after = shifted(weights, "section", -1).astype(jnp.float32)
    return (BEFORE_SHARE * before + AFTER_SHARE * after).astype(jnp.bfloat16)


def general_body(entering, w_query, w_keyval, w_out):
    rows = entering[0].astype(jnp.float32)
    features = rows.shape[1] * lax.axis_size("tensor")
    square_total = lax.psum(jnp.sum(rows * rows, axis=-1, keepdims=True), "tensor")
    normed = (rows * lax.rsqrt(square_total / features + EPSILON)).astype(jnp.bfloat16)
    normed = lax.all_gather(normed, "tensor", axis=1, tiled=True)
    length = normed.shape[0]
    query_weight = lax.all_gather(rebuilt(w_query)[0], "fsdp", axis=0, tiled=True)
    keyval_weight = lax.all_gather(rebuilt(w_keyval)[0], "fsdp", axis=0, tiled=True)
    out_weight = lax.all_gather(rebuilt(w_out)[0], "fsdp", axis=1, tiled=True)
    kv_count = keyval_weight.shape[1]
    raw = jnp.dot(normed, query_weight, preferred_element_type=jnp.float32)
    raw = raw.reshape(length, kv_count, -1, HEAD_DIM)
    keyval_raw = jnp.dot(
        normed, keyval_weight.reshape(features, -1), preferred_element_type=jnp.float32
    ).reshape(length, kv_count, 2 * HEAD_DIM)
    cosine, sine = rope_tables(length, HEAD_DIM)
    queries = head_norm_rope(raw, cosine[:, None, None], sine[:, None, None]).astype(jnp.bfloat16)
    keys = head_norm_rope(
        keyval_raw[..., :HEAD_DIM], cosine[:, None], sine[:, None]
    ).astype(jnp.bfloat16)
    values = keyval_raw[..., HEAD_DIM:].astype(jnp.bfloat16)
    causal = jnp.arange(length)[:, None] >= jnp.arange(length)[None, :]

    def one_group(query_slice):
        scores = jnp.einsum("qkd,pkd->kqp", query_slice, keys, preferred_element_type=jnp.float32)
        expo = jnp.exp(scores * (1.0 / math.sqrt(HEAD_DIM)) - math.sqrt(HEAD_DIM))
        expo = jnp.where(causal[None], expo, 0.0)
        weights = (expo / jnp.sum(expo, axis=-1, keepdims=True)).astype(jnp.bfloat16)
        return jnp.einsum(
            "kqp,pkd->qkd", weights, values, preferred_element_type=jnp.float32
        ).astype(jnp.bfloat16)

    mixed = lax.map(one_group, jnp.moveaxis(queries, 2, 0))
    mixed = jnp.moveaxis(mixed, 0, 2).reshape(length, -1)
    terms = jnp.dot(mixed, out_weight, preferred_element_type=jnp.float32).astype(jnp.bfloat16)
    summed = lax.psum_scatter(terms, "tensor", scatter_dimension=1, tiled=True)
    return (rows + summed.astype(jnp.float32)).astype(jnp.bfloat16)[None]


def solution(mesh):
    in_specs = (
        P("section", "fsdp", "tensor"),
        P("section", "fsdp", "tensor"),
        P("section", "fsdp", "tensor", None),
        P("section", "tensor", "fsdp"),
    )
    out_specs = P("section", "fsdp", "tensor")

    def step(entering, w_query, w_keyval, w_out):
        chunked = (
            mesh.shape["section"] % 2 == 0
            and mesh.shape["fsdp"] == 2
            and mesh.shape["tensor"] == 4
            and w_keyval.shape[2] == mesh.shape["tensor"]
            and w_keyval.shape[3] == 2 * HEAD_DIM
            and w_query.shape[2] % (mesh.shape["tensor"] * QUERY_CHUNKS * HEAD_DIM) == 0
            and w_out.shape[2] % (mesh.shape["tensor"] * OUT_CHUNKS * LANES) == 0
        )
        return jax.shard_map(
            body if chunked else general_body,
            mesh=mesh,
            in_specs=in_specs,
            out_specs=out_specs,
            check_vma=False,
        )(entering, w_query, w_keyval, w_out)

    return step
```

```python
import functools
import math

import jax
import jax.numpy as jnp
import numpy as np
from jax import lax
from jax.experimental import pallas as pl
from jax.experimental.pallas import tpu as pltpu
from jax.sharding import PartitionSpec as P

HEAD_DIM = 128
EPSILON = 1e-06
ROPE_BASE = 1000000.0
BEFORE_SHARE = 0.6
AFTER_SHARE = 0.4
LANES = 128
VMEM_BYTES = 48 * 1024 * 1024
QUERY_CHUNKS = 4
OUT_CHUNKS = 4
FIRST = (1, 3)
STEPS = (('G', 1, 'n1', 6000), ('G', 2, '', 6000), ('C', 0, '', 700), ('G', 3, '', 6000), ('C', 1, '', 4000), ('X', 0, '', 200), ('G', 4, '', 6000), ('C', 2, '', 0), ('G', 5, 'y0', 6000), ('C', 3, 'y1', 4000), ('K', 0, '', 6000), ('G', 6, '', 6000), ('C', 4, '', 0), ('A', 1, 'a1', 0), ('A', 2, 'a3', 2000), ('A', 3, '', 1000), ('C', 5, '', 4000), ('A', 4, '', 2000), ('G', 8, '', 6000), ('G', 7, '', 6000), ('C', 6, '', 0), ('P', 5, '', 3000), ('C', 7, '', 4000), ('R', 5, 'y3', 1000), ('P', 6, '', 6000), ('C', 8, '', 0), ('P', 7, 't5', 3000), ('R', 6, 'y4', 50), ('R', 7, '', 1000), ('Q', 8, 'a2', 4000))

SMEM = pl.BlockSpec(memory_space=pltpu.SMEM)
VMEM = pl.BlockSpec(memory_space=pltpu.VMEM)


def estimate(cost):
    return pl.CostEstimate(flops=cost * 2**20, bytes_accessed=0, transcendentals=0)


def params():
    return pltpu.CompilerParams(vmem_limit_bytes=VMEM_BYTES)


def rope_tables(length, width):
    inverse = ROPE_BASE ** (np.arange(width // 2) * (-2.0 / width))
    angles = np.arange(length)[:, None] * inverse[None, :]
    cosine, sine = np.cos(angles), np.sin(angles)
    cosine, sine = np.concatenate([cosine, cosine], 1), np.concatenate([-sine, sine], 1)
    return jnp.asarray(cosine, jnp.float32), jnp.asarray(sine, jnp.float32)


ANY = pl.BlockSpec(memory_space=pl.ANY)


def combine_kernel(shares, near, far, *rest):
    out = rest[-1]
    mixed = shares[0] * near[...].astype(jnp.float32) + shares[1] * far[...].astype(jnp.float32)
    out[...] = mixed.astype(out.dtype)


def combine(shares, near, far, near_block, width, after=(), cost=0):
    rows, columns = far.shape
    step = min(rows, 512)
    block = pl.BlockSpec((step, width), lambda i, j: (i, j))
    return pl.pallas_call(
        combine_kernel,
        out_shape=jax.ShapeDtypeStruct(far.shape, far.dtype),
        grid=(rows // step, columns // width),
        in_specs=[SMEM, pl.BlockSpec((step, width), lambda i, j: (i, near_block(j))), block]
        + [ANY] * len(after),
        out_specs=block,
        compiler_params=params(),
        cost_estimate=estimate(cost),
    )(shares, near, far, *after)


def columns_kernel(whole, *rest):
    rest[-1][...] = whole[...]


def columns_of(whole, block, width, pieces, after=(), cost=0):
    rows = whole.shape[0]
    step = min(rows, 512)
    return pl.pallas_call(
        columns_kernel,
        out_shape=jax.ShapeDtypeStruct((rows, pieces * width), whole.dtype),
        grid=(rows // step, pieces),
        in_specs=[pl.BlockSpec((step, width), lambda i, j: (i, block(j)))] + [ANY] * len(after),
        out_specs=pl.BlockSpec((step, width), lambda i, j: (i, j)),
        compiler_params=params(),
        cost_estimate=estimate(cost),
    )(whole, *after)


def copy_kernel(source, *rest):
    rest[-1][...] = source[...]


def copied(array, after, cost=0):
    return pl.pallas_call(
        copy_kernel,
        out_shape=jax.ShapeDtypeStruct(array.shape, array.dtype),
        in_specs=[VMEM] + [ANY] * len(after),
        out_specs=VMEM,
        compiler_params=params(),
        cost_estimate=estimate(cost),
    )(array, *after)


def project(ids, blocks, own, other, whole):
    half = own.shape[0]
    mine, place, count = ids[0], ids[1], len(blocks)
    whole[pl.ds(pl.multiple_of(mine * half, half), half), :] = own[...]
    whole[pl.ds(pl.multiple_of((1 - mine) * half, half), half), :] = other[...]
    total = None
    for k, block in enumerate(blocks):
        width = block.shape[1]
        owner = lax.rem(place - k + count, count)
        rows = pl.ds(pl.multiple_of(owner * width, width), width)
        term = jnp.dot(block[...], whole[rows, :], preferred_element_type=jnp.float32)
        total = term if total is None else total + term
    return total


def norm_rope(vectors, cosine, signed_sine):
    meansq = jnp.mean(vectors * vectors, axis=-1, keepdims=True)
    normed = vectors * lax.rsqrt(meansq + EPSILON)
    return normed * cosine + pltpu.roll(normed, HEAD_DIM // 2, 1) * signed_sine


def keyval_kernel(count, ids, *refs):
    blocks = refs[:count]
    own, other, cosine, sine = refs[count : count + 4]
    keys, values, scales, whole = refs[-4:]
    total = 0.0
    features = 0
    for block in blocks:
        rows = block[...].astype(jnp.float32)
        total = total + jnp.sum(rows * rows, axis=-1, keepdims=True)
        features += block.shape[1]
    scale = lax.rsqrt(total / features + EPSILON)
    raw = project(ids, blocks, own, other, whole) * scale
    keys[...] = norm_rope(raw[:, :HEAD_DIM], cosine[...], sine[...]).astype(keys.dtype)
    values[...] = raw[:, HEAD_DIM:].astype(values.dtype)
    scales[...] = jnp.broadcast_to(scale, scales.shape)


def keyval(ids, blocks, own, other, cosine, sine, after=(), cost=0):
    length = blocks[0].shape[0]
    features = sum(b.shape[1] for b in blocks)
    head = jax.ShapeDtypeStruct((length, HEAD_DIM), jnp.bfloat16)
    return pl.pallas_call(
        functools.partial(keyval_kernel, len(blocks)),
        out_shape=(head, head, jax.ShapeDtypeStruct((length, LANES), jnp.float32)),
        in_specs=[SMEM] + [VMEM] * (len(blocks) + 4) + [ANY] * len(after),
        out_specs=(VMEM,) * 3,
        scratch_shapes=[pltpu.VMEM((features, own.shape[1]), own.dtype)],
        compiler_params=params(),
        cost_estimate=estimate(cost),
    )(ids, *blocks, own, other, cosine, sine, *after)


def attend_kernel(count, ids, *refs):
    blocks = refs[:count]
    own, other, keys, values, scales, cosine, sine = refs[count : count + 7]
    mixed, whole = refs[-2:]
    raw = project(ids, blocks, own, other, whole)
    length = raw.shape[0]
    rows = length // 2 if length % 16 == 0 else length
    scale = scales[:, :1]
    for head in range(raw.shape[1] // HEAD_DIM):
        columns = slice(head * HEAD_DIM, (head + 1) * HEAD_DIM)
        query = norm_rope(raw[:, columns] * scale, cosine[...], sine[...]).astype(jnp.bfloat16)
        for first in range(0, length, rows):
            last = first + rows
            scores = lax.dot_general(
                query[first:last],
                keys[:last, :],
                (((1,), (1,)), ((), ())),
                preferred_element_type=jnp.float32,
            )
            expo = jnp.exp(scores * (1.0 / math.sqrt(HEAD_DIM)) - math.sqrt(HEAD_DIM))
            at = first + lax.broadcasted_iota(jnp.int32, expo.shape, 0)
            expo = jnp.where(lax.broadcasted_iota(jnp.int32, expo.shape, 1) <= at, expo, 0.0)
            total = jnp.sum(expo, axis=-1, keepdims=True)
            product = jnp.dot(
                expo.astype(jnp.bfloat16), values[:last, :], preferred_element_type=jnp.float32
            )
            mixed[first:last, columns] = (product / total).astype(mixed.dtype)


def attend(ids, blocks, own, other, keys, values, scales, cosine, sine, after=(), cost=0):
    length = blocks[0].shape[0]
    features = sum(b.shape[1] for b in blocks)
    width = own.shape[1]
    return pl.pallas_call(
        functools.partial(attend_kernel, len(blocks)),
        out_shape=jax.ShapeDtypeStruct((length, width), jnp.bfloat16),
        in_specs=[SMEM] + [VMEM] * (len(blocks) + 7) + [ANY] * len(after),
        out_specs=VMEM,
        scratch_shapes=[pltpu.VMEM((features, width), own.dtype)],
        compiler_params=params(),
        cost_estimate=estimate(cost),
    )(ids, *blocks, own, other, keys, values, scales, cosine, sine, *after)


def products(ids, mixed, own, other, by_owner):
    mine = ids[0]
    count, _, width = by_owner.shape
    per_half = count // 2
    rows = jnp.concatenate([part[...] for part in mixed], axis=1)
    for half, weights in ((mine, own), (1 - mine, other)):
        total = jnp.dot(rows, weights[...], preferred_element_type=jnp.float32)
        for piece in range(per_half):
            by_owner[half * per_half + piece] = total[
                :, piece * width : (piece + 1) * width
            ].astype(by_owner.dtype)


def partial_kernel(count, parts, ids, *refs):
    kept, sent, by_owner = refs[-3:]
    products(ids, refs[:parts], refs[parts], refs[parts + 1], by_owner)
    low = lax.rem(ids[1], 2)
    for pair in range(count // 2):
        kept[pair] = by_owner[2 * pair + low]
        sent[pair] = by_owner[2 * pair + 1 - low]


def direct_kernel(count, parts, ids, *refs):
    outs, by_owner = refs[-1 - count : -1], refs[-1]
    products(ids, refs[:parts], refs[parts], refs[parts + 1], by_owner)
    for k in range(count):
        outs[k][...] = by_owner[lax.rem(ids[1] + k, count)]


def direct_partials(ids, mixed, own, other, count, after=(), cost=0):
    length = mixed[0].shape[0]
    width = 2 * own.shape[1] // count
    piece = jax.ShapeDtypeStruct((length, width), jnp.bfloat16)
    return pl.pallas_call(
        functools.partial(direct_kernel, count, len(mixed)),
        out_shape=(piece,) * count,
        in_specs=[SMEM] + [VMEM] * (len(mixed) + 2) + [ANY] * len(after),
        out_specs=(VMEM,) * count,
        scratch_shapes=[pltpu.VMEM((count, length, width), jnp.bfloat16)],
        compiler_params=params(),
        cost_estimate=estimate(cost),
    )(ids, *mixed, own, other, *after)


def partials(ids, mixed, own, other, count, after=(), cost=0):
    length = mixed[0].shape[0]
    width = 2 * own.shape[1] // count
    half = jax.ShapeDtypeStruct((count // 2, length, width), jnp.bfloat16)
    return pl.pallas_call(
        functools.partial(partial_kernel, count, len(mixed)),
        out_shape=(half, half),
        in_specs=[SMEM] + [VMEM] * (len(mixed) + 2) + [ANY] * len(after),
        out_specs=(VMEM, VMEM),
        scratch_shapes=[pltpu.VMEM((count, length, width), jnp.bfloat16)],
        compiler_params=params(),
        cost_estimate=estimate(cost),
    )(ids, *mixed, own, other, *after)


def reduce_kernel(ids, kept, got, *refs):
    still, sent = refs[-2:]
    high = lax.rem(lax.div(ids[1], 2), 2)
    still[...] = kept[high].astype(jnp.float32) + got[high].astype(jnp.float32)
    away = kept[1 - high].astype(jnp.float32) + got[1 - high].astype(jnp.float32)
    sent[...] = away.astype(sent.dtype)


def reduce(ids, kept, got, after=(), cost=0):
    shape = kept.shape[1:]
    return pl.pallas_call(
        reduce_kernel,
        out_shape=(
            jax.ShapeDtypeStruct(shape, jnp.float32),
            jax.ShapeDtypeStruct(shape, jnp.bfloat16),
        ),
        in_specs=[SMEM, VMEM, VMEM] + [ANY] * len(after),
        out_specs=(VMEM, VMEM),
        compiler_params=params(),
        cost_estimate=estimate(cost),
    )(ids, kept, got, *after)


def leave_kernel(counts, rows, *refs):
    out = refs[-1]
    width = rows.shape[1] // len(counts)
    first = 0
    for chunk, count in enumerate(counts):
        columns = slice(chunk * width, (chunk + 1) * width)
        total = rows[:, columns].astype(jnp.float32)
        for piece in refs[first : first + count]:
            total = total + piece[...].astype(jnp.float32)
        first += count
        out[:, columns] = total.astype(out.dtype)


def leave(rows, pieces):
    flat = [piece for chunk in pieces for piece in chunk]
    return pl.pallas_call(
        functools.partial(leave_kernel, [len(chunk) for chunk in pieces]),
        out_shape=jax.ShapeDtypeStruct(rows.shape, rows.dtype),
        in_specs=[VMEM] * (1 + len(flat)),
        out_specs=VMEM,
        compiler_params=params(),
        cost_estimate=estimate(1),
    )(rows, *flat)


def permute(array, axis, source):
    count = lax.axis_size(axis)
    return lax.ppermute(array, axis, [(source(i) % count, i) for i in range(count)])


def from_near(array):
    return permute(array, "section", lambda i: i ^ 1)


def from_far(array):
    return permute(array, "section", lambda i: i + 1 if i % 2 else i - 1)


def from_other_half(array):
    return permute(array, "fsdp", lambda i: i ^ 1)


def body(entering, w_query, w_keyval, w_out):
    count = lax.axis_size("tensor")
    section = lax.axis_index("section")
    ids = jnp.stack([lax.axis_index("fsdp"), lax.axis_index("tensor")]).astype(jnp.int32)
    shares = jnp.where(
        section % 2 == 0,
        jnp.array([AFTER_SHARE, BEFORE_SHARE], jnp.float32),
        jnp.array([BEFORE_SHARE, AFTER_SHARE], jnp.float32),
    )
    rows = entering[0]
    length = rows.shape[0]
    own_query = w_query[0]
    own_keyval = w_keyval.reshape(w_keyval.shape[1], -1)
    own_out = w_out[0]
    query_width = own_query.shape[1] // QUERY_CHUNKS
    halves = count // 2
    quarter = own_out.shape[1] // halves
    out_width = quarter // OUT_CHUNKS

    near_keyval, near_query, near_out = map(from_near, (own_keyval, own_query, own_out))
    far = {0: from_far(own_keyval)}
    places = [(own_keyval, near_keyval, own_keyval.shape[1], lambda j: 0)]
    for c in range(QUERY_CHUNKS):
        places.append((own_query, near_query, query_width, lambda j, c=c: c))
    for c in range(OUT_CHUNKS):
        places.append((own_out, near_out, out_width, lambda j, c=c: j * OUT_CHUNKS + c))
    pieces_of = [1] * (1 + QUERY_CHUNKS) + [halves] * OUT_CHUNKS
    blocks = [rows] + [None] * (count - 1)
    for k in FIRST:
        blocks[k] = permute(rows, "tensor", lambda i, k=k: i - k)
    cosine, sine = rope_tables(length, HEAD_DIM)

    own, other, mixed, halves_of, pieces, before = {}, {}, [], {}, {}, []
    for kind, c, arrivals, cost in STEPS:
        after = list(before)
        for name in arrivals.split():
            if name[0] == "y":
                after.append(other[int(name[1:])])
            elif name[0] == "a":
                after.append(blocks[int(name[1:])])
            elif name[0] == "n":
                after.append((near_query, near_out)[int(name[1:])])
            elif name[0] == "s":
                after.append(halves_of[int(name[1:])][1])
            else:
                after.append(pieces[int(name[1:])][1])
        if kind == "G":
            whole, _, width, place = places[c]
            chunk = columns_of(whole, place, width, pieces_of[c], after=after, cost=cost)
            far[c] = from_far(chunk)
            before = [chunk]
        elif kind == "C":
            _, near, width, place = places[c]
            own[c] = combine(shares, near, far[c], place, width, after=after, cost=cost)
            other[c] = from_other_half(own[c])
            before = [own[c]]
        elif kind == "X":
            again = copied(rows, after=after + [blocks[k] for k in FIRST], cost=cost)
            for k in range(1, count):
                if k not in FIRST:
                    blocks[k] = permute(again, "tensor", lambda i, k=k: i - k)
            before = [again]
        elif kind == "K":
            keys, values, scales = keyval(
                ids, blocks, own[c], other[c], cosine, sine, after=after, cost=cost
            )
            before = [scales]
        elif kind == "A":
            mixed.append(
                attend(
                    ids,
                    blocks,
                    own[c],
                    other[c],
                    keys,
                    values,
                    scales,
                    cosine,
                    sine,
                    after=after,
                    cost=cost,
                )
            )
            before = [mixed[-1]]
        elif kind == "P":
            kept, sent = partials(
                ids, mixed, own[c], other[c], count, after=after, cost=cost
            )
            halves_of[c] = (kept, permute(sent, "tensor", lambda i: i ^ 1))
            before = [kept]
        elif kind == "Q":
            parts = direct_partials(
                ids, mixed, own[c], other[c], count, after=after, cost=cost
            )
            pieces[c] = [parts[0]] + [
                permute(parts[k], "tensor", lambda i, k=k: i - k) for k in sorted(range(1, count), key=lambda k: -min(k, count - k))
            ]
            before = [parts[0]]
        else:
            kept, sent = reduce(ids, *halves_of[c], after=after, cost=cost)
            pieces[c] = (kept, permute(sent, "tensor", lambda i: i ^ 2))
            before = [kept]
    pieces = [pieces[c] for c in sorted(pieces)]
    return leave(rows, pieces)[None]


def shifted(block, axis, distance):
    return permute(block, axis, lambda i: i - distance)


def head_norm_rope(vectors, cosine, signed_sine):
    meansq = jnp.mean(vectors * vectors, axis=-1, keepdims=True)
    normed = vectors * lax.rsqrt(meansq + EPSILON)
    return normed * cosine + jnp.roll(normed, vectors.shape[-1] // 2, axis=-1) * signed_sine


def rebuilt(weights):
    before = shifted(weights, "section", 1).astype(jnp.float32)
    after = shifted(weights, "section", -1).astype(jnp.float32)
    return (BEFORE_SHARE * before + AFTER_SHARE * after).astype(jnp.bfloat16)


def general_body(entering, w_query, w_keyval, w_out):
    rows = entering[0].astype(jnp.float32)
    features = rows.shape[1] * lax.axis_size("tensor")
    square_total = lax.psum(jnp.sum(rows * rows, axis=-1, keepdims=True), "tensor")
    normed = (rows * lax.rsqrt(square_total / features + EPSILON)).astype(jnp.bfloat16)
    normed = lax.all_gather(normed, "tensor", axis=1, tiled=True)
    length = normed.shape[0]
    query_weight = lax.all_gather(rebuilt(w_query)[0], "fsdp", axis=0, tiled=True)
    keyval_weight = lax.all_gather(rebuilt(w_keyval)[0], "fsdp", axis=0, tiled=True)
    out_weight = lax.all_gather(rebuilt(w_out)[0], "fsdp", axis=1, tiled=True)
    kv_count = keyval_weight.shape[1]
    raw = jnp.dot(normed, query_weight, preferred_element_type=jnp.float32)
    raw = raw.reshape(length, kv_count, -1, HEAD_DIM)
    keyval_raw = jnp.dot(
        normed, keyval_weight.reshape(features, -1), preferred_element_type=jnp.float32
    ).reshape(length, kv_count, 2 * HEAD_DIM)
    cosine, sine = rope_tables(length, HEAD_DIM)
    queries = head_norm_rope(raw, cosine[:, None, None], sine[:, None, None]).astype(jnp.bfloat16)
    keys = head_norm_rope(
        keyval_raw[..., :HEAD_DIM], cosine[:, None], sine[:, None]
    ).astype(jnp.bfloat16)
    values = keyval_raw[..., HEAD_DIM:].astype(jnp.bfloat16)
    causal = jnp.arange(length)[:, None] >= jnp.arange(length)[None, :]

    def one_group(query_slice):
        scores = jnp.einsum("qkd,pkd->kqp", query_slice, keys, preferred_element_type=jnp.float32)
        expo = jnp.exp(scores * (1.0 / math.sqrt(HEAD_DIM)) - math.sqrt(HEAD_DIM))
        expo = jnp.where(causal[None], expo, 0.0)
        weights = (expo / jnp.sum(expo, axis=-1, keepdims=True)).astype(jnp.bfloat16)
        return jnp.einsum(
            "kqp,pkd->qkd", weights, values, preferred_element_type=jnp.float32
        ).astype(jnp.bfloat16)

    mixed = lax.map(one_group, jnp.moveaxis(queries, 2, 0))
    mixed = jnp.moveaxis(mixed, 0, 2).reshape(length, -1)
    terms = jnp.dot(mixed, out_weight, preferred_element_type=jnp.float32).astype(jnp.bfloat16)
    summed = lax.psum_scatter(terms, "tensor", scatter_dimension=1, tiled=True)
    return (rows + summed.astype(jnp.float32)).astype(jnp.bfloat16)[None]


def solution(mesh):
    in_specs = (
        P("section", "fsdp", "tensor"),
        P("section", "fsdp", "tensor"),
        P("section", "fsdp", "tensor", None),
        P("section", "tensor", "fsdp"),
    )
    out_specs = P("section", "fsdp", "tensor")

    def step(entering, w_query, w_keyval, w_out):
        chunked = (
            mesh.shape["section"] % 2 == 0
            and mesh.shape["fsdp"] == 2
            and mesh.shape["tensor"] == 4
            and w_keyval.shape[2] == mesh.shape["tensor"]
            and w_keyval.shape[3] == 2 * HEAD_DIM
            and w_query.shape[2] % (mesh.shape["tensor"] * QUERY_CHUNKS * HEAD_DIM) == 0
            and w_out.shape[2] % (mesh.shape["tensor"] * OUT_CHUNKS * LANES) == 0
        )
        return jax.shard_map(
            body if chunked else general_body,
            mesh=mesh,
            in_specs=in_specs,
            out_specs=out_specs,
            check_vma=False,
        )(entering, w_query, w_keyval, w_out)

    return step
```
